512 devices in a mesh: tm: 128 (over y, x, z_lo), chan: 4 (over z_hi, core).
Axes of the slice: x: 4, y: 8, z: 8 (z_hi: 2, z_lo: 4; z = z_hi * 4 + z_lo), core: 2. Of those that a mesh axis runs over, the one named last changes fastest.
Arguments:
- voltages: bfloat16 [32, 2, 2, 512, 16384], P('chan', None, None, 'tm'), parts along dimension 0, may hold values from -6 to 6
- taps: float32 [4, 16384], replicated, may hold values from -3 to 3
Outputs:
- drift_power: float32 [8, 16, 131072], P('chan', None, 'tm'), parts along dimension 0
The draws below stay inside these ranges and needn't reach their ends.
There are 4 independent parts, one for each index of `chan`. The reference program is written for one: setup_inputs(seed, part) draws one part's arguments, and reference() takes and returns one part's arrays. A program takes and returns all parts, laid end to end along the dimension named above; an argument that names none is the same for every part. Nothing has to cross between parts.
All inputs are finite; a program needn't handle non-finite values.
Results may differ from the reference program's by a relative error of at most 0.0017.
The reference program's roundings to bfloat16 on the way (of `filtered` and `turned`) count: a program that leaves them out, or rounds other values in their place, can miss the bound.
Values may be sent and summed in bfloat16 or wider, within the bound.
No kernel may reach another device: no remote copies, remote signals or barrier semaphores. Data moves between devices by JAX's collectives and lax.ppermute only.
A program may use at most 64 MiB of HBM per device.

```python
import math
import jax
import jax.numpy as jnp
from jax import lax

CC = 8
FR_DEV = 4
TAPS = 4
NT = 16
NFFT = 16384
FRAMES = 512
N_TM = 128


def shard_levels(rng, dims, shards, smallest, top_value):
    level = 1.0
    for axis_at, blocks in shards:
        draws = jax.random.uniform(jax.random.fold_in(jax.random.fold_in(rng, 6), axis_at), (blocks,), jnp.float32, smallest / len(shards), top_value / len(shards))
        level = level * jnp.repeat(jnp.exp(draws), dims[axis_at] // blocks).reshape((-1,) + (1,) * (len(dims) - 1 - axis_at))
    return level


def bell_draw(stream_key, extent, scale, most, pieces=(), held_as=jnp.bfloat16):
    gain = shard_levels(stream_key, extent, pieces, -0.22, 0.18) if pieces else 1.0
    result = jax.random.normal(stream_key, extent, jnp.float32) * scale * gain
    return jnp.minimum(jnp.maximum(result, -most), most).astype(held_as)


def setup_inputs(seed: int = 0, part: int = 0) -> dict:
    splits = jax.random.split(jax.random.key(seed), 3)
    part_keys = jax.random.split(jax.random.fold_in(splits[2], part), 3)
    return {
        "voltages": bell_draw(part_keys[0], (CC, 2, 2, FRAMES, NFFT), 1.0, 6.0, ((3, 128),)),
        "taps": bell_draw(splits[1], (TAPS, NFFT), 0.5, 3.0, (), jnp.float32),
    }


def section_table(size):
    index = jnp.arange(size, dtype=jnp.int32)
    product = index[:, None] * index[None, :] % size
    angle = -2.0 * math.pi / size * product.astype(jnp.float32)
    scale = 1.0 / math.sqrt(size)
    real_part = jnp.cos(angle) * scale
    imag_part = jnp.sin(angle) * scale
    top = jnp.stack([real_part, -imag_part], axis=1)
    low = jnp.stack([imag_part, real_part], axis=1)
    return jnp.stack([top, low], axis=0).astype(jnp.bfloat16)

def twiddle_table(size):
    index = jnp.arange(size, dtype=jnp.int32)
    product = index[:, None] * index[None, :]
    angle = -2.0 * math.pi / (size * size) * product.astype(jnp.float32)
    return (jnp.cos(angle), jnp.sin(angle))

def spectra(extended, taps, frames):
    count = taps.shape[0]
    length = taps.shape[1]
    side = math.isqrt(length)
    sample = jnp.arange(length, dtype=jnp.int32)
    shaped = taps * (1.0 - 2.0 * (sample % 2).astype(jnp.float32))
    filtered = shaped[0] * extended[:, :, :, count - 1:count - 1 + frames, :].astype(jnp.float32)
    for k in range(1, count):
        filtered = filtered + shaped[k] * extended[:, :, :, count - 1 - k:count - 1 - k + frames, :].astype(jnp.float32)
    filtered = filtered.astype(jnp.bfloat16)
    shape = filtered.shape
    filtered = filtered.reshape(shape[0], shape[1], shape[2], frames, side, side)
    table = section_table(side)
    first = jnp.einsum('ukvn,abvfnm->abfukm', table.astype(jnp.float32), filtered.astype(jnp.float32), precision=lax.Precision.HIGHEST)
    cos_part, sin_part = twiddle_table(side)
    real_part = first[:, :, :, 0]
    imag_part = first[:, :, :, 1]
    turned = jnp.stack([real_part * cos_part - imag_part * sin_part, real_part * sin_part + imag_part * cos_part], axis=3).astype(jnp.bfloat16)
    spectrum = jnp.einsum('ujvm,abfvkm->fabujk', table.astype(jnp.float32), turned.astype(jnp.float32), precision=lax.Precision.HIGHEST)
    power = lax.optimization_barrier(jnp.sum(spectrum * spectrum, axis=(2, 3)))
    return power.reshape(frames, shape[0] * length)

def taylor(padded, sense):
    level = padded[:, None, :]
    length = 1
    while level.shape[0] > 1:
        earlier = level[0::2]
        later = level[1::2]
        rows = []
        for drift in range(2 * length):
            half = drift // 2
            move = drift - half
            rows.append(earlier[:, half] + jnp.roll(later[:, half], -sense * move, axis=-1))
        level = jnp.stack(rows, axis=1)
        length = length * 2
    return level[0]

def reference(voltages, taps):
    count = taps.shape[0]
    history = jnp.zeros(voltages.shape[:3] + (count - 1, voltages.shape[4]), jnp.bfloat16)
    padded = jnp.concatenate([history, voltages], axis=3)

    def one_block(block):
        start = (block * FR_DEV).astype(jnp.int32)
        extended = lax.dynamic_slice_in_dim(padded, start, FR_DEV + count - 1, 3)
        return spectra(extended, taps, FR_DEV)
    power = lax.map(one_block, jnp.arange(N_TM, dtype=jnp.int32))
    power = power.reshape(FR_DEV * N_TM, power.shape[2])
    steps_power = power.reshape(NT, -1, power.shape[1]).sum(axis=1) / (FR_DEV * N_TM // NT)
    zeros = jnp.zeros((NT, NT), jnp.float32)
    widened = jnp.concatenate([zeros, steps_power, zeros], axis=1)
    rising = taylor(widened, 1)[:, NT:NT + steps_power.shape[1]]
    falling = taylor(widened, -1)[:, NT:NT + steps_power.shape[1]]
    return jnp.stack([rising, falling], axis=0) / NT
```

```python
import math

import jax
import jax.numpy as jnp
import ml_dtypes
import numpy as np
from jax import lax
from jax.experimental import pallas as pl
from jax.experimental.pallas import tpu as pltpu
from jax.sharding import PartitionSpec as P

NT = 16
SIDE = 128
BLOCK = 16


def tables(side):
    index = np.arange(side, dtype=np.int64)
    angle = -2.0 * math.pi / side * ((index[:, None] * index[None, :]) % side)
    re = (np.cos(angle) / math.sqrt(side)).astype(ml_dtypes.bfloat16)
    im = (np.sin(angle) / math.sqrt(side)).astype(ml_dtypes.bfloat16)
    fourier = np.block([[re, -im], [im, re]])
    turn = -2.0 * math.pi / (side * side) * (index[:, None] * index[None, :])
    return fourier, np.cos(turn).astype(np.float32), np.sin(turn).astype(np.float32)


def pack_kernel(v_ref, out_ref, rows):
    frames = v_ref.shape[3] // SIDE
    for p in range(2):
        for r in range(2):
            rows[...] = v_ref[0, p, r].astype(jnp.float32)
            for t in range(1, frames):
                out_ref[p, r, t - 1] = rows[pl.ds(t, SIDE, stride=frames), :].astype(jnp.bfloat16)


def chunk_power(v_ref, h_ref, taps_ref, fourier_ref, back_ref, cos_ref, sin_ref, rows, wide, tall):
    frames = v_ref.shape[3] // SIDE
    count = taps_ref.shape[0] // SIDE
    lane = lax.broadcasted_iota(jnp.int32, (BLOCK, SIDE), 1)
    sign = 1.0 - 2.0 * (lane % 2).astype(jnp.float32)
    total = None
    for p in range(2):
        for r in range(2):
            rows[r] = v_ref[0, p, r].astype(jnp.float32)
        for n in range(0, SIDE, BLOCK):
            shaped = [
                taps_ref[pl.ds(count * n + k, BLOCK, stride=count), :] * sign for k in range(count)
            ]
            for r in range(2):
                frame = [h_ref[p, r, t, pl.ds(n, BLOCK), :].astype(jnp.float32) for t in range(count - 1)]
                frame += [rows[r, pl.ds(frames * n + t, BLOCK, stride=frames), :] for t in range(frames)]
                for t in range(frames):
                    value = shaped[0] * frame[t + count - 1]
                    for k in range(1, count):
                        value = value + shaped[k] * frame[t + count - 1 - k]
                    wide[pl.ds(r * SIDE + n, BLOCK), pl.ds(t * SIDE, SIDE)] = value.astype(jnp.bfloat16)
        first = jnp.dot(fourier_ref[...], wide[...], preferred_element_type=jnp.float32)
        cos, sin = cos_ref[...], sin_ref[...]
        for t in range(frames):
            re = first[:SIDE, t * SIDE : (t + 1) * SIDE]
            im = first[SIDE:, t * SIDE : (t + 1) * SIDE]
            tall[pl.ds(t * SIDE, SIDE), pl.ds(0, SIDE)] = (re * cos - im * sin).astype(jnp.bfloat16)
            tall[pl.ds(t * SIDE, SIDE), pl.ds(SIDE, SIDE)] = (re * sin + im * cos).astype(jnp.bfloat16)
        spectrum = jnp.dot(tall[...], back_ref[...], preferred_element_type=jnp.float32)
        square = spectrum * spectrum
        for t in range(frames):
            part = square[t * SIDE : (t + 1) * SIDE]
            part = part[:, :SIDE] + part[:, SIDE:]
            total = part if total is None else total + part
    return total.T


def chunk_kernel(*refs):
    ins, (out_ref,), scratch = refs[:7], refs[7:8], refs[8:]
    out_ref[...] = chunk_power(*ins, *scratch)


def last_kernel(*refs):
    ins, before, out_ref, scratch = refs[:7], refs[7:-4], refs[-4], refs[-3:]
    last = chunk_power(*ins, *scratch)
    each = SIDE // 8
    tiles = []
    for ref in before:
        tiles += [ref[pl.ds(8 * i, 8), :] for i in range(each)]
    tiles += [last[8 * i : 8 * i + 8] for i in range(each)]
    zero = jnp.zeros((8, SIDE), jnp.float32)
    row = lax.broadcasted_iota(jnp.int32, (8, SIDE), 0)
    for d in range(len(tiles)):
        after = tiles[d + 1] if d + 1 < len(tiles) else zero
        prior = tiles[d - 1] if d else zero
        edge = jnp.where(row == 0, after, jnp.where(row == 7, prior, 0.0))
        out_ref[d] = jnp.concatenate([tiles[d], edge], axis=0).astype(jnp.bfloat16)


def tree_kernel(in_ref, out_ref, flat):
    sources = in_ref.shape[0]
    per = sources // NT
    lane = lax.broadcasted_iota(jnp.int32, (16, SIDE), 1)
    steps = []
    for s in range(NT):
        value = in_ref[s * per].astype(jnp.float32)
        for i in range(1, per):
            value = value + in_ref[s * per + i].astype(jnp.float32)
        steps.append(value)

    def moved(value, move, sense):
        if move == 0:
            return value
        if sense > 0:
            here = pltpu.roll(value, SIDE - move, 1)
            return jnp.where(lane < SIDE - move, here, pltpu.roll(here, 15, 0))
        here = pltpu.roll(value, move, 1)
        return jnp.where(lane >= move, here, pltpu.roll(here, 1, 0))

    for which, sense in enumerate((1, -1)):
        level = [[value] for value in steps]
        length = 1
        while len(level) > 1:
            level = [
                [
                    level[j][d // 2] + moved(level[j + 1][d // 2], d - d // 2, sense)
                    for d in range(2 * length)
                ]
                for j in range(0, len(level), 2)
            ]
            length *= 2
        for d in range(NT):
            flat[pl.ds(8 * d, 8), :] = level[0][d][:8]
        for r in range(8):
            out_ref[which, :, pl.ds(r * SIDE, SIDE)] = flat[pl.ds(r, NT, stride=8), :] * (1.0 / (4 * per * NT))


def per_device(voltages, taps):
    channels, _, _, frames, length = voltages.shape
    count = taps.shape[0]
    peers = lax.axis_size("tm")
    fourier, cos, sin = tables(SIDE)
    back = jnp.asarray(np.ascontiguousarray(fourier.T))
    fourier, cos, sin = jnp.asarray(fourier), jnp.asarray(cos), jnp.asarray(sin)
    rows = voltages.reshape(channels, 2, 2, frames, SIDE, SIDE).transpose(0, 1, 2, 4, 3, 5)
    rows = rows.reshape(channels, 2, 2, SIDE * frames, SIDE)
    coefficients = taps.reshape(count, SIDE, SIDE).transpose(1, 0, 2).reshape(SIDE * count, SIDE)
    pairs = [(i, i + 1) for i in range(peers - 1)]

    def block_of(c):
        return pl.BlockSpec((1, 2, 2, SIDE * frames, SIDE), lambda i: (c, 0, 0, 0, 0))

    def whole(shape):
        return pl.BlockSpec(shape, lambda i: (0,) * len(shape))

    halo = (2, 2, count - 1, SIDE, SIDE)
    near = []
    for c in range(channels):
        packed = pl.pallas_call(
            pack_kernel,
            grid=(1,),
            in_specs=[block_of(c)],
            out_specs=whole(halo),
            out_shape=jax.ShapeDtypeStruct(halo, jnp.bfloat16),
            scratch_shapes=[pltpu.VMEM((SIDE * frames, SIDE), jnp.float32)],
            cost_estimate=pl.CostEstimate(flops=1 << 20, bytes_accessed=1 << 20, transcendentals=0),
            name="pack",
        )(rows)
        near.append(lax.ppermute(packed, "tm", pairs))

    constants = [coefficients, fourier, back, cos, sin]
    specs = [whole(value.shape) for value in constants]
    scratch = [
        pltpu.VMEM((2, SIDE * frames, SIDE), jnp.float32),
        pltpu.VMEM((2 * SIDE, frames * SIDE), jnp.bfloat16),
        pltpu.VMEM((frames * SIDE, 2 * SIDE), jnp.bfloat16),
    ]
    cost = pl.CostEstimate(flops=300 << 20, bytes_accessed=2 << 20, transcendentals=0)
    tile = (SIDE, SIDE)
    powers = []
    for c in range(channels - 1):
        powers.append(
            pl.pallas_call(
                chunk_kernel,
                grid=(1,),
                in_specs=[block_of(c), whole(halo)] + specs,
                out_specs=whole(tile),
                out_shape=jax.ShapeDtypeStruct(tile, jnp.float32),
                scratch_shapes=scratch,
                cost_estimate=cost,
                name="chunk",
            )(rows, near[c], *constants)
        )
    sent = (peers, 16, SIDE)
    out = pl.pallas_call(
        last_kernel,
        grid=(1,),
        in_specs=[block_of(channels - 1), whole(halo)] + specs + [whole(tile)] * (channels - 1),
        out_specs=whole(sent),
        out_shape=jax.ShapeDtypeStruct(sent, jnp.bfloat16),
        scratch_shapes=scratch,
        cost_estimate=cost,
        name="last",
    )(rows, near[channels - 1], *constants, *powers)
    owned = lax.all_to_all(out, "tm", split_axis=0, concat_axis=0, tiled=True)
    result = (2, NT, channels * length // peers)
    return pl.pallas_call(
        tree_kernel,
        grid=(1,),
        in_specs=[whole(sent)],
        out_specs=whole(result),
        out_shape=jax.ShapeDtypeStruct(result, jnp.float32),
        scratch_shapes=[pltpu.VMEM((8 * NT, SIDE), jnp.float32)],
        cost_estimate=pl.CostEstimate(flops=1 << 22, bytes_accessed=1 << 20, transcendentals=0),
        name="tree",
    )(owned)


def solution(mesh):
    placed = (P("chan", None, None, "tm", None), P())
    return jax.shard_map(
        per_device, mesh=mesh, in_specs=placed, out_specs=P("chan", None, "tm"), check_vma=False
    )
```

```python
import math

import jax
import jax.numpy as jnp
import ml_dtypes
import numpy as np
from jax import lax
from jax.experimental import pallas as pl
from jax.experimental.pallas import tpu as pltpu
from jax.sharding import PartitionSpec as P

NT = 16
SIDE = 128
BLOCK = 16
SENT = 10
VMEM = pltpu.CompilerParams(vmem_limit_bytes=12 << 20)


def tables(side):
    index = np.arange(side, dtype=np.int64)
    angle = -2.0 * math.pi / side * ((index[:, None] * index[None, :]) % side)
    re = (np.cos(angle) / math.sqrt(side)).astype(ml_dtypes.bfloat16)
    im = (np.sin(angle) / math.sqrt(side)).astype(ml_dtypes.bfloat16)
    fourier = np.block([[re, -im], [im, re]])
    turn = -2.0 * math.pi / (side * side) * (index[:, None] * index[None, :])
    return fourier, np.cos(turn).astype(np.float32), np.sin(turn).astype(np.float32)


def pack_kernel(v_ref, out_ref, rows):
    frames = v_ref.shape[3] // SIDE
    for p in range(2):
        for r in range(2):
            rows[...] = v_ref[0, p, r].astype(jnp.float32)
            for t in range(1, frames):
                out_ref[p, r, t - 1] = rows[pl.ds(t, SIDE, stride=frames), :].astype(jnp.bfloat16)


def chunk_power(v_ref, h_ref, taps_ref, fourier_ref, back_ref, cos_ref, sin_ref, rows, wide, tall):
    frames = v_ref.shape[3] // SIDE
    count = taps_ref.shape[0] // SIDE
    lane = lax.broadcasted_iota(jnp.int32, (BLOCK, SIDE), 1)
    sign = 1.0 - 2.0 * (lane % 2).astype(jnp.float32)
    total = None
    for p in range(2):
        for r in range(2):
            rows[r] = v_ref[0, p, r].astype(jnp.float32)
        for n in range(0, SIDE, BLOCK):
            shaped = [
                taps_ref[pl.ds(count * n + k, BLOCK, stride=count), :] * sign for k in range(count)
            ]
            for r in range(2):
                frame = [h_ref[p, r, t, pl.ds(n, BLOCK), :].astype(jnp.float32) for t in range(count - 1)]
                frame += [rows[r, pl.ds(frames * n + t, BLOCK, stride=frames), :] for t in range(frames)]
                for t in range(frames):
                    value = shaped[0] * frame[t + count - 1]
                    for k in range(1, count):
                        value = value + shaped[k] * frame[t + count - 1 - k]
                    wide[pl.ds(r * SIDE + n, BLOCK), pl.ds(t * SIDE, SIDE)] = value.astype(jnp.bfloat16)
        first = jnp.dot(fourier_ref[...], wide[...], preferred_element_type=jnp.float32)
        cos, sin = cos_ref[...], sin_ref[...]
        for t in range(frames):
            re = first[:SIDE, t * SIDE : (t + 1) * SIDE]
            im = first[SIDE:, t * SIDE : (t + 1) * SIDE]
            tall[pl.ds(t * SIDE, SIDE), pl.ds(0, SIDE)] = (re * cos - im * sin).astype(jnp.bfloat16)
            tall[pl.ds(t * SIDE, SIDE), pl.ds(SIDE, SIDE)] = (re * sin + im * cos).astype(jnp.bfloat16)
        spectrum = jnp.dot(tall[...], back_ref[...], preferred_element_type=jnp.float32)
        square = spectrum * spectrum
        for t in range(frames):
            part = square[t * SIDE : (t + 1) * SIDE]
            part = part[:, :SIDE] + part[:, SIDE:]
            total = part if total is None else total + part
    return total.T


def chunk_kernel(*refs):
    ins, (out_ref,), scratch = refs[:7], refs[7:8], refs[8:]
    out_ref[...] = chunk_power(*ins, *scratch)


def last_kernel(*refs):
    ins, before, out_ref, scratch, every, apart = refs[:7], refs[7:-6], refs[-6], refs[-5:-2], refs[-2], refs[-1]
    for c, ref in enumerate(before):
        every[pl.ds(c * SIDE, SIDE), :] = ref[...]
    every[pl.ds(len(before) * SIDE, SIDE), :] = chunk_power(*ins, *scratch)
    peers = apart.shape[0] // SENT
    for j in range(8):
        apart[pl.ds(j, peers, stride=SENT), :] = every[pl.ds(j, peers, stride=8), :]
    apart[pl.ds(8, peers - 1, stride=SENT), :] = every[pl.ds(8, peers - 1, stride=8), :]
    apart[pl.ds(SENT + 9, peers - 1, stride=SENT), :] = every[pl.ds(7, peers - 1, stride=8), :]
    apart[pl.ds(SENT * (peers - 1) + 8, 1), :] = jnp.zeros((1, SIDE), jnp.float32)
    apart[pl.ds(9, 1), :] = jnp.zeros((1, SIDE), jnp.float32)
    out_ref[...] = apart[...].astype(jnp.bfloat16)


def tree_kernel(in_ref, out_ref, wide, steps, flat):
    per = in_ref.shape[0] // SENT // NT
    lane = lax.broadcasted_iota(jnp.int32, (16, SIDE), 1)
    wide[...] = in_ref[...].astype(jnp.float32)
    steps[...] = jnp.zeros(steps.shape, jnp.float32)
    for j in range(SENT):
        value = wide[pl.ds(j, NT, stride=SENT * per), :]
        for i in range(1, per):
            value = value + wide[pl.ds(SENT * i + j, NT, stride=SENT * per), :]
        steps[pl.ds(15 if j == 9 else j, NT, stride=16), :] = value

    def moved(value, move, sense):
        if move == 0:
            return value
        if sense > 0:
            here = pltpu.roll(value, SIDE - move, 1)
            return jnp.where(lane < SIDE - move, here, pltpu.roll(here, 15, 0))
        here = pltpu.roll(value, move, 1)
        return jnp.where(lane >= move, here, pltpu.roll(here, 1, 0))

    for which, sense in enumerate((1, -1)):
        level = [[steps[pl.ds(16 * s, 16), :]] for s in range(NT)]
        length = 1
        while len(level) > 1:
            level = [
                [
                    level[j][d // 2] + moved(level[j + 1][d // 2], d - d // 2, sense)
                    for d in range(2 * length)
                ]
                for j in range(0, len(level), 2)
            ]
            length *= 2
        for d in range(NT):
            flat[pl.ds(8 * d, 8), :] = level[0][d][:8]
        for r in range(8):
            out_ref[which, :, pl.ds(r * SIDE, SIDE)] = flat[pl.ds(r, NT, stride=8), :] * (1.0 / (4 * per * NT))


def per_device(voltages, taps):
    channels, _, _, frames, length = voltages.shape
    count = taps.shape[0]
    peers = lax.axis_size("tm")
    fourier, cos, sin = tables(SIDE)
    back = jnp.asarray(np.ascontiguousarray(fourier.T))
    fourier, cos, sin = jnp.asarray(fourier), jnp.asarray(cos), jnp.asarray(sin)
    rows = voltages.reshape(channels, 2, 2, frames, SIDE, SIDE).transpose(0, 1, 2, 4, 3, 5)
    rows = rows.reshape(channels, 2, 2, SIDE * frames, SIDE)
    coefficients = taps.reshape(count, SIDE, SIDE).transpose(1, 0, 2).reshape(SIDE * count, SIDE)
    pairs = [(i, i + 1) for i in range(peers - 1)]

    def block_of(c):
        return pl.BlockSpec((1, 2, 2, SIDE * frames, SIDE), lambda i: (c, 0, 0, 0, 0))

    def whole(shape):
        return pl.BlockSpec(shape, lambda i: (0,) * len(shape))

    halo = (2, 2, count - 1, SIDE, SIDE)
    near = []
    for c in range(channels):
        packed = pl.pallas_call(
            pack_kernel,
            grid=(1,),
            in_specs=[block_of(c)],
            out_specs=whole(halo),
            out_shape=jax.ShapeDtypeStruct(halo, jnp.bfloat16),
            scratch_shapes=[pltpu.VMEM((SIDE * frames, SIDE), jnp.float32)],
            compiler_params=VMEM,
        cost_estimate=pl.CostEstimate(flops=1 << 20, bytes_accessed=1 << 20, transcendentals=0),
            name="pack",
        )(rows)
        near.append(lax.ppermute(packed, "tm", pairs))

    constants = [coefficients, fourier, back, cos, sin]
    specs = [whole(value.shape) for value in constants]
    scratch = [
        pltpu.VMEM((2, SIDE * frames, SIDE), jnp.float32),
        pltpu.VMEM((2 * SIDE, frames * SIDE), jnp.bfloat16),
        pltpu.VMEM((frames * SIDE, 2 * SIDE), jnp.bfloat16),
    ]
    cost = pl.CostEstimate(flops=300 << 20, bytes_accessed=2 << 20, transcendentals=0)
    tile = (SIDE, SIDE)
    powers = []
    for c in range(channels - 1):
        powers.append(
            pl.pallas_call(
                chunk_kernel,
                grid=(1,),
                in_specs=[block_of(c), whole(halo)] + specs,
                out_specs=whole(tile),
                out_shape=jax.ShapeDtypeStruct(tile, jnp.float32),
                scratch_shapes=scratch,
                compiler_params=VMEM,
                cost_estimate=cost,
                name="chunk",
            )(rows, near[c], *constants)
        )
    sent = (peers * SENT, SIDE)
    out = pl.pallas_call(
        last_kernel,
        grid=(1,),
        in_specs=[block_of(channels - 1), whole(halo)] + specs + [whole(tile)] * (channels - 1),
        out_specs=whole(sent),
        out_shape=jax.ShapeDtypeStruct(sent, jnp.bfloat16),
        scratch_shapes=scratch
        + [pltpu.VMEM((channels * SIDE, SIDE), jnp.float32), pltpu.VMEM(sent, jnp.float32)],
        compiler_params=VMEM,
        cost_estimate=cost,
        name="last",
    )(rows, near[channels - 1], *constants, *powers)
    pairs_of_rows = out.reshape(peers, SENT // 2, 2, SIDE)
    owned = lax.all_to_all(pairs_of_rows, "tm", split_axis=0, concat_axis=0, tiled=True).reshape(sent)
    result = (2, NT, channels * length // peers)
    return pl.pallas_call(
        tree_kernel,
        grid=(1,),
        in_specs=[whole(sent)],
        out_specs=whole(result),
        out_shape=jax.ShapeDtypeStruct(result, jnp.float32),
        scratch_shapes=[
            pltpu.VMEM(sent, jnp.float32),
            pltpu.VMEM((16 * NT, SIDE), jnp.float32),
            pltpu.VMEM((8 * NT, SIDE), jnp.float32),
        ],
        compiler_params=VMEM,
        cost_estimate=pl.CostEstimate(flops=1 << 22, bytes_accessed=1 << 20, transcendentals=0),
        name="tree",
    )(owned)


def solution(mesh):
    placed = (P("chan", None, None, "tm", None), P())
    return jax.shard_map(
        per_device, mesh=mesh, in_specs=placed, out_specs=P("chan", None, "tm"), check_vma=False
    )
```

```python
import math

import jax
import jax.numpy as jnp
import ml_dtypes
import numpy as np
from jax import lax
from jax.experimental import pallas as pl
from jax.experimental.pallas import tpu as pltpu
from jax.sharding import Mesh
from jax.sharding import PartitionSpec as P

NT = 16
SIDE = 128
BLOCK = 16
AHEAD = 4
SENT = 9
PARAMS = pltpu.CompilerParams(vmem_limit_bytes=12 << 20)
FIRST = pltpu.CompilerParams(vmem_limit_bytes=63_000_000)
VMEM = pl.BlockSpec(memory_space=pltpu.VMEM)
ANY = pl.BlockSpec(memory_space=pl.ANY)


def tables(side):
    index = np.arange(side, dtype=np.int64)
    angle = -2.0 * math.pi / side * ((index[:, None] * index[None, :]) % side)
    re = (np.cos(angle) / math.sqrt(side)).astype(ml_dtypes.bfloat16)
    im = (np.sin(angle) / math.sqrt(side)).astype(ml_dtypes.bfloat16)
    fourier = np.block([[re, -im], [im, re]])
    turn = -2.0 * math.pi / (side * side) * (index[:, None] * index[None, :])
    return fourier, np.cos(turn).astype(np.float32), np.sin(turn).astype(np.float32)


def channel_at(place, half):
    lower = place + 4 if place < 4 else 3 if place == 4 else place - 5
    return lower + half * (place - lower)


def receiver_half():
    half, last = lax.axis_index("half"), lax.axis_size("tm") - 1
    return jnp.where((half == 0) & (lax.axis_index("tm") == last), 1, half)


def spread(value, rows, out_ref, p, r):
    frames = value.shape[0] // SIDE
    rows[...] = value.astype(jnp.float32)
    for t in range(1, frames):
        out_ref[p, r, t - 1] = rows[pl.ds(t, SIDE, stride=frames), :].astype(jnp.bfloat16)


def first_pack_kernel(v_ref, out_ref, block, rows, sems):
    channel = channel_at(0, receiver_half())
    copies = {}
    for p in range(2):
        for r in range(2):
            copies[p, r] = pltpu.make_async_copy(v_ref.at[channel, p, r], block.at[p, r], sems.at[p, r])
            copies[p, r].start()
    for p in range(2):
        for r in range(2):
            copies[p, r].wait()
            spread(block[p, r], rows.at[p, r], out_ref, p, r)


def pack_kernel(place, pols, v_ref, out_ref, rows):
    channel = channel_at(place, receiver_half())
    for i, p in enumerate(pols):
        for r in range(2):
            spread(v_ref[channel, p, r], rows.at[r], out_ref, i, r)


def chunk_power(place, pols, ins, scratch):
    v_ref, h_ref, taps_ref, fourier_ref, back_ref, cos_ref, sin_ref = ins
    rows, wide, tall = scratch
    channel = channel_at(place, lax.axis_index("half"))
    frames = v_ref.shape[3] // SIDE
    count = taps_ref.shape[0] // SIDE
    lane = lax.broadcasted_iota(jnp.int32, (BLOCK, SIDE), 1)
    sign = 1.0 - 2.0 * (lane % 2).astype(jnp.float32)
    total = None
    for i, p in enumerate(pols):
        for r in range(2):
            rows[r] = v_ref[channel, p, r].astype(jnp.float32)
        for n in range(0, SIDE, BLOCK):
            shaped = [
                taps_ref[pl.ds(count * n + k, BLOCK, stride=count), :] * sign for k in range(count)
            ]
            for r in range(2):
                frame = [h_ref[i, r, t, pl.ds(n, BLOCK), :].astype(jnp.float32) for t in range(count - 1)]
                frame += [rows[r, pl.ds(frames * n + t, BLOCK, stride=frames), :] for t in range(frames)]
                for t in range(frames):
                    value = shaped[0] * frame[t + count - 1]
                    for k in range(1, count):
                        value = value + shaped[k] * frame[t + count - 1 - k]
                    wide[pl.ds(r * SIDE + n, BLOCK), pl.ds(t * SIDE, SIDE)] = value.astype(jnp.bfloat16)
        first = jnp.dot(fourier_ref[...], wide[...], preferred_element_type=jnp.float32)
        cos, sin = cos_ref[...], sin_ref[...]
        for t in range(frames):
            re = first[:SIDE, t * SIDE : (t + 1) * SIDE]
            im = first[SIDE:, t * SIDE : (t + 1) * SIDE]
            tall[pl.ds(t * SIDE, SIDE), pl.ds(0, SIDE)] = (re * cos - im * sin).astype(jnp.bfloat16)
            tall[pl.ds(t * SIDE, SIDE), pl.ds(SIDE, SIDE)] = (re * sin + im * cos).astype(jnp.bfloat16)
        spectrum = jnp.dot(tall[...], back_ref[...], preferred_element_type=jnp.float32)
        square = spectrum * spectrum
        for t in range(frames):
            part = square[t * SIDE : (t + 1) * SIDE]
            part = part[:, :SIDE] + part[:, SIDE:]
            total = part if total is None else total + part
    return total


def chunk_kernel(place, *refs):
    ins, out_ref, scratch = refs[:7], refs[7], refs[8:]
    out_ref[...] = chunk_power(place, (0, 1), ins, scratch).T


def first_half_kernel(place, *refs):
    ins, out_ref, scratch = refs[:7], refs[7], refs[8:]
    out_ref[...] = chunk_power(place, (0,), ins, scratch)


def lay_out(every, apart, peers, step, start):
    for j in range(8):
        apart[pl.ds(start + j, peers, stride=step), :] = every[pl.ds(8 + j, peers, stride=8), :]
    lane = lax.broadcasted_iota(jnp.int32, (peers, SIDE), 1)
    after = every[pl.ds(16, peers, stride=8), :]
    before = every[pl.ds(7, peers, stride=8), :]
    apart[pl.ds(start + 8, peers, stride=step), :] = jnp.where(lane < SIDE // 2, after, before)


def ends(every, before, after):
    count = every.shape[0]
    every[pl.ds(0, 8), :] = before
    every[pl.ds(count - 8, 8), :] = after


def ship_kernel(p0, p1, p2, p3, border, out_ref):
    half = lax.axis_index("half")
    zero = jnp.zeros((8, SIDE), jnp.float32)
    before = jnp.where(half == 0, border[pl.ds(SIDE - 8, 8), :], zero)
    after = jnp.where(half == 1, border[pl.ds(0, 8), :], zero)
    out_ref[pl.ds(0, 16), :] = jnp.concatenate([zero, before], axis=0).astype(jnp.bfloat16)
    for i, ref in enumerate((p0, p1, p2, p3)):
        out_ref[pl.ds(16 + i * SIDE, SIDE), :] = ref[...].astype(jnp.bfloat16)
    out_ref[pl.ds(16 + 4 * SIDE, 16), :] = jnp.concatenate([after, zero], axis=0).astype(jnp.bfloat16)


def last_kernel(place, *refs):
    ins, (part, p0, p3, border, p5, p6, theirs, relayed), out_ref = refs[:7], refs[7:15], refs[15]
    scratch, (every, apart, plain) = refs[16:19], refs[19:]
    half = lax.axis_index("half")
    peers = apart.shape[0] // (2 * SENT)
    plain[...] = theirs[...].astype(jnp.float32) + relayed[...].astype(jnp.float32)
    lay_out(plain.at[pl.ds(8, plain.shape[0] - 16)], apart, peers, 2 * SENT, SENT)

    def put(slot, value):
        every[pl.ds(pl.multiple_of(8 + slot * SIDE, 8), SIDE), :] = value

    put(3 * (1 - half), border[...])
    put(half, p5[...])
    put(1 + half, p6[...])
    zero = jnp.zeros((8, SIDE), jnp.float32)
    ends(
        every,
        jnp.where(half == 1, p3[pl.ds(SIDE - 8, 8), :], zero),
        jnp.where(half == 0, p0[pl.ds(0, 8), :], zero),
    )
    put(2 + half, (part[...] + chunk_power(place, (1,), ins, scratch)).T)
    lay_out(every, apart, peers, 2 * SENT, 0)
    out_ref[...] = apart[...].astype(jnp.bfloat16)


def tree_kernel(scale, in_ref, out_ref, wide, steps, flat):
    half = lax.axis_index("half")
    step = 2 * SENT
    sources = in_ref.shape[0] // step
    per = sources // (NT // 2)
    lane = lax.broadcasted_iota(jnp.int32, (16, SIDE), 1)
    wide[...] = in_ref[...].astype(jnp.float32)
    steps[...] = jnp.zeros(steps.shape, jnp.float32)
    for whose in range(2):
        base = 8 * 16 * (half if whose == 0 else 1 - half)
        for j in range(SENT):
            value = wide[pl.ds(whose * SENT + j, 8, stride=step * per), :]
            for i in range(1, per):
                value = value + wide[pl.ds(step * i + whose * SENT + j, 8, stride=step * per), :]
            for row in (j,) if j < 8 else (8, 15):
                if whose == 0:
                    steps[pl.ds(base + row, 8, stride=16), :] = value
                else:
                    steps[pl.ds(base + 6 * 16 + row, 2, stride=16), :] = value[:2]
                    steps[pl.ds(base + row, 6, stride=16), :] = value[2:]

    def moved(value, move, sense):
        if move == 0:
            return value
        if sense > 0:
            here = pltpu.roll(value, SIDE - move, 1)
            return jnp.where(lane < SIDE - move, here, pltpu.roll(here, 15, 0))
        here = pltpu.roll(value, move, 1)
        return jnp.where(lane >= move, here, pltpu.roll(here, 1, 0))

    for which, sense in enumerate((1, -1)):
        level = [[steps[pl.ds(16 * s, 16), :]] for s in range(NT)]
        length = 1
        while len(level) > 1:
            level = [
                [
                    level[j][d // 2] + moved(level[j + 1][d // 2], d - d // 2, sense)
                    for d in range(2 * length)
                ]
                for j in range(0, len(level), 2)
            ]
            length *= 2
        for d in range(NT):
            flat[pl.ds(8 * d, 8), :] = level[0][d][:8]
        for r in range(8):
            out_ref[which, :, pl.ds(r * SIDE, SIDE)] = flat[pl.ds(r, NT, stride=8), :] * scale


def call(body, name, args, shape, dtype, scratch, flops=1 << 20, after=(), specs=None, params=PARAMS):
    def ordered(*refs):
        body(*refs[: len(args)], *refs[len(args) + len(after) :])

    return pl.pallas_call(
        ordered,
        in_specs=(specs or [VMEM] * len(args)) + [ANY] * len(after),
        out_specs=VMEM,
        out_shape=jax.ShapeDtypeStruct(shape, dtype),
        scratch_shapes=scratch,
        compiler_params=params,
        cost_estimate=pl.CostEstimate(flops=flops, bytes_accessed=1 << 20, transcendentals=0),
        name=name,
    )(*args, *after)


def bind(body, *first):
    def bound(*refs):
        body(*first, *refs)

    return bound


def per_device(voltages, taps):
    channels, _, _, frames, length = voltages.shape
    count = taps.shape[0]
    peers = lax.axis_size("tm")
    f32, bf16 = jnp.float32, jnp.bfloat16
    fourier, cos, sin = tables(SIDE)
    back = jnp.asarray(np.ascontiguousarray(fourier.T))
    fourier, cos, sin = jnp.asarray(fourier), jnp.asarray(cos), jnp.asarray(sin)
    rows = voltages.reshape(channels, 2, 2, frames, SIDE, SIDE).transpose(0, 1, 2, 4, 3, 5)
    rows = rows.reshape(channels, 2, 2, SIDE * frames, SIDE)
    coefficients = taps.reshape(count, SIDE, SIDE).transpose(1, 0, 2).reshape(SIDE * count, SIDE)
    pairs = [(i, i + 1) for i in range(2 * peers - 1)]
    tile = (SIDE, SIDE)

    halo = (2, 2, count - 1, SIDE, SIDE)
    interleaved = (SIDE * frames, SIDE)
    first = call(
        first_pack_kernel,
        "pack_first",
        [rows],
        halo,
        bf16,
        [
            pltpu.VMEM((2, 2) + interleaved, bf16),
            pltpu.VMEM((2, 2) + interleaved, f32),
            pltpu.SemaphoreType.DMA((2, 2)),
        ],
        specs=[ANY],
        params=FIRST,
    )
    packs = [first]
    near = [lax.ppermute(first, ("half", "tm"), pairs)]

    def send(place, pols, after):
        shape = (len(pols),) + halo[1:]
        body = bind(pack_kernel, place, pols)
        value = call(body, "pack", [rows], shape, bf16, [pltpu.VMEM((2,) + interleaved, f32)], after=after)
        packs.append(value)
        near.append(lax.ppermute(value, ("half", "tm"), pairs))

    constants = [coefficients, fourier, back, cos, sin]
    scratch = [
        pltpu.VMEM((2,) + interleaved, f32),
        pltpu.VMEM((2 * SIDE, frames * SIDE), bf16),
        pltpu.VMEM((frames * SIDE, 2 * SIDE), bf16),
    ]
    flops = 300 << 20
    for place in range(1, AHEAD):
        send(place, (0, 1), [first])
    power = []
    last = channels - 1
    for place in range(last):
        args = [rows, near[place], *constants]
        power.append(call(bind(chunk_kernel, place), "chunk", args, tile, f32, scratch, flops, after=power[-1:]))
        if place + AHEAD < last:
            send(place + AHEAD, (0, 1), power[-1:])
        elif place + AHEAD == last:
            send(last, (0,), power[-1:])
            send(last, (1,), power[-1:])
    args = [rows, near[last], *constants]
    part = call(bind(first_half_kernel, last), "chunk_half", args, tile, f32, scratch, flops // 2, after=power[-1:])
    plane = 2 * peers // channels
    shipped = (16 + channels // 2 * SIDE + 16, SIDE)
    ship = call(ship_kernel, "ship", power[:5], shipped, bf16, [], after=[packs[-1]])
    across, edge = [], (channels // 2 - 1) * plane + plane - 1
    for i in range(2 * peers):
        half, at = divmod(i, peers)
        across.append((i, (1 - half) * peers + (at + plane) % peers))
    straight = [pair for pair in across if pair[0] != edge]
    target = dict(across)[edge]
    beside = edge - 4
    theirs = lax.ppermute(ship, ("half", "tm"), straight)
    relayed = lax.ppermute(ship, ("half", "tm"), [(edge, beside)])
    relayed = lax.ppermute(relayed, ("half", "tm"), [(beside, target)])
    every = pltpu.VMEM((8 + 4 * SIDE + 8, SIDE), f32)
    sent = (2 * peers * SENT, SIDE)
    out = call(
        bind(last_kernel, last),
        "last",
        [rows, near[last + 1], *constants, part, power[0], power[3], power[4], power[5], power[6], theirs, relayed],
        sent,
        bf16,
        scratch + [every, pltpu.VMEM(sent, f32), pltpu.VMEM(shipped, f32)],
        flops // 2,
    )
    out = out.reshape(peers, SENT, 2, SIDE)
    owned = lax.all_to_all(out, "tm", split_axis=0, concat_axis=0, tiled=True).reshape(sent)
    scale = 1.0 / (frames * 2 * peers)
    return call(
        bind(tree_kernel, scale),
        "tree",
        [owned],
        (2, NT, channels * length // (2 * peers)),
        f32,
        [pltpu.VMEM(sent, f32), pltpu.VMEM((16 * NT, SIDE), f32), pltpu.VMEM((8 * NT, SIDE), f32)],
    )


def solution(mesh):
    peers, groups = mesh.shape["tm"], mesh.shape["chan"]
    halves = Mesh(mesh.devices.reshape(2, peers // 2, groups), ("half", "tm", "chan"))
    split = ("half", "tm")
    placed = (P("chan", None, None, split, None), P())
    return jax.shard_map(per_device, mesh=halves, in_specs=placed, out_specs=P("chan", None, split), check_vma=False)
```

```python
import math

import jax
import jax.numpy as jnp
import ml_dtypes
import numpy as np
from jax import lax
from jax.experimental import pallas as pl
from jax.experimental.pallas import tpu as pltpu
from jax.sharding import Mesh
from jax.sharding import PartitionSpec as P

NT = 16
SIDE = 128
BLOCK = 16
AHEAD = 4
SENT = 9
PARAMS = pltpu.CompilerParams(vmem_limit_bytes=12 << 20)
FIRST = pltpu.CompilerParams(vmem_limit_bytes=56_000_000)
VMEM = pl.BlockSpec(memory_space=pltpu.VMEM)
ANY = pl.BlockSpec(memory_space=pl.ANY)


def tables(side):
    index = np.arange(side, dtype=np.int64)
    angle = -2.0 * math.pi / side * ((index[:, None] * index[None, :]) % side)
    re = (np.cos(angle) / math.sqrt(side)).astype(ml_dtypes.bfloat16)
    im = (np.sin(angle) / math.sqrt(side)).astype(ml_dtypes.bfloat16)
    fourier = np.block([[re, -im], [im, re]])
    turn = -2.0 * math.pi / (side * side) * (index[:, None] * index[None, :])
    return fourier, np.cos(turn).astype(np.float32), np.sin(turn).astype(np.float32)


def channel_at(place, half):
    lower = place + 4 if place < 4 else 3 if place == 4 else place - 5
    return lower + half * (place - lower)


def receiver_half():
    half, last = lax.axis_index("half"), lax.axis_size("tm") - 1
    return jnp.where((half == 0) & (lax.axis_index("tm") == last), 1, half)


def spread(value, rows, out_ref, p, r):
    frames = value.shape[0] // SIDE
    rows[...] = value.astype(jnp.float32)
    for t in range(1, frames):
        out_ref[p, r, t - 1] = rows[pl.ds(t, SIDE, stride=frames), :].astype(jnp.bfloat16)


def first_pack_kernel(v_ref, out_ref, block, rows, sems):
    channel = channel_at(0, receiver_half())
    copies = {}
    for p in range(2):
        for r in range(2):
            copies[p, r] = pltpu.make_async_copy(v_ref.at[channel, p, r], block.at[p, r], sems.at[p, r])
            copies[p, r].start()
    for p in range(2):
        for r in range(2):
            copies[p, r].wait()
            spread(block[p, r], rows.at[p, r], out_ref, p, r)


def pack_kernel(place, pols, v_ref, out_ref, rows):
    channel = channel_at(place, receiver_half())
    for i, p in enumerate(pols):
        for r in range(2):
            spread(v_ref[channel, p, r], rows.at[r], out_ref, i, r)


def chunk_power(place, pols, ins, scratch):
    v_ref, h_ref, taps_ref, fourier_ref, back_ref, cos_ref, sin_ref = ins
    rows, wide, tall = scratch
    channel = channel_at(place, lax.axis_index("half"))
    frames = v_ref.shape[3] // SIDE
    count = taps_ref.shape[0] // SIDE
    lane = lax.broadcasted_iota(jnp.int32, (BLOCK, SIDE), 1)
    sign = 1.0 - 2.0 * (lane % 2).astype(jnp.float32)
    total = None
    for i, p in enumerate(pols):
        for r in range(2):
            rows[r] = v_ref[channel, p, r].astype(jnp.float32)
        for n in range(0, SIDE, BLOCK):
            shaped = [
                taps_ref[pl.ds(count * n + k, BLOCK, stride=count), :] * sign for k in range(count)
            ]
            for r in range(2):
                frame = [h_ref[i, r, t, pl.ds(n, BLOCK), :].astype(jnp.float32) for t in range(count - 1)]
                frame += [rows[r, pl.ds(frames * n + t, BLOCK, stride=frames), :] for t in range(frames)]
                for t in range(frames):
                    value = shaped[0] * frame[t + count - 1]
                    for k in range(1, count):
                        value = value + shaped[k] * frame[t + count - 1 - k]
                    wide[pl.ds(r * SIDE + n, BLOCK), pl.ds(t * SIDE, SIDE)] = value.astype(jnp.bfloat16)
        first = jnp.dot(fourier_ref[...], wide[...], preferred_element_type=jnp.float32)
        cos, sin = cos_ref[...], sin_ref[...]
        for t in range(frames):
            re = first[:SIDE, t * SIDE : (t + 1) * SIDE]
            im = first[SIDE:, t * SIDE : (t + 1) * SIDE]
            tall[pl.ds(t * SIDE, SIDE), pl.ds(0, SIDE)] = (re * cos - im * sin).astype(jnp.bfloat16)
            tall[pl.ds(t * SIDE, SIDE), pl.ds(SIDE, SIDE)] = (re * sin + im * cos).astype(jnp.bfloat16)
        spectrum = jnp.dot(tall[...], back_ref[...], preferred_element_type=jnp.float32)
        square = spectrum * spectrum
        for t in range(frames):
            part = square[t * SIDE : (t + 1) * SIDE]
            part = part[:, :SIDE] + part[:, SIDE:]
            total = part if total is None else total + part
    return total


def chunk_kernel(place, *refs):
    ins, out_ref, scratch = refs[:7], refs[7], refs[8:]
    out_ref[...] = chunk_power(place, (0, 1), ins, scratch).T


def first_half_kernel(place, *refs):
    ins, out_ref, scratch = refs[:7], refs[7], refs[8:]
    out_ref[...] = chunk_power(place, (0,), ins, scratch)


def lay_out(every, apart, peers, step, start):
    for j in range(8):
        apart[pl.ds(start + j, peers, stride=step), :] = every[pl.ds(8 + j, peers, stride=8), :]
    lane = lax.broadcasted_iota(jnp.int32, (peers, SIDE), 1)
    after = every[pl.ds(16, peers, stride=8), :]
    before = every[pl.ds(7, peers, stride=8), :]
    apart[pl.ds(start + 8, peers, stride=step), :] = jnp.where(lane < SIDE // 2, after, before)


def ends(every, before, after):
    count = every.shape[0]
    every[pl.ds(0, 8), :] = before
    every[pl.ds(count - 8, 8), :] = after


def ship_kernel(p0, p1, p2, p3, border, out_ref):
    half = lax.axis_index("half")
    zero = jnp.zeros((8, SIDE), jnp.float32)
    before = jnp.where(half == 0, border[pl.ds(SIDE - 8, 8), :], zero)
    after = jnp.where(half == 1, border[pl.ds(0, 8), :], zero)
    out_ref[pl.ds(0, 16), :] = jnp.concatenate([zero, before], axis=0).astype(jnp.bfloat16)
    for i, ref in enumerate((p0, p1, p2, p3)):
        out_ref[pl.ds(16 + i * SIDE, SIDE), :] = ref[...].astype(jnp.bfloat16)
    out_ref[pl.ds(16 + 4 * SIDE, 16), :] = jnp.concatenate([after, zero], axis=0).astype(jnp.bfloat16)


def last_kernel(place, *refs):
    ins, (part, p0, p3, border, p5, p6, theirs, relayed), out_ref = refs[:7], refs[7:15], refs[15]
    scratch, (every, apart, plain) = refs[16:19], refs[19:]
    half = lax.axis_index("half")
    peers = apart.shape[0] // (2 * SENT)
    plain[...] = theirs[...].astype(jnp.float32) + relayed[...].astype(jnp.float32)
    lay_out(plain.at[pl.ds(8, plain.shape[0] - 16)], apart, peers, 2 * SENT, SENT)

    def put(slot, value):
        every[pl.ds(pl.multiple_of(8 + slot * SIDE, 8), SIDE), :] = value

    put(3 * (1 - half), border[...])
    put(half, p5[...])
    put(1 + half, p6[...])
    zero = jnp.zeros((8, SIDE), jnp.float32)
    ends(
        every,
        jnp.where(half == 1, p3[pl.ds(SIDE - 8, 8), :], zero),
        jnp.where(half == 0, p0[pl.ds(0, 8), :], zero),
    )
    put(2 + half, (part[...] + chunk_power(place, (1,), ins, scratch)).T)
    lay_out(every, apart, peers, 2 * SENT, 0)
    out_ref[...] = apart[...].astype(jnp.bfloat16)


def tree_kernel(scale, in_ref, out_ref, wide, steps, flat):
    half = lax.axis_index("half")
    step = 2 * SENT
    sources = in_ref.shape[0] // step
    per = sources // (NT // 2)
    lane = lax.broadcasted_iota(jnp.int32, (16, SIDE), 1)
    wide[...] = in_ref[...].astype(jnp.float32)
    steps[...] = jnp.zeros(steps.shape, jnp.float32)
    for whose in range(2):
        base = 8 * 16 * (half if whose == 0 else 1 - half)
        for j in range(SENT):
            value = wide[pl.ds(whose * SENT + j, 8, stride=step * per), :]
            for i in range(1, per):
                value = value + wide[pl.ds(step * i + whose * SENT + j, 8, stride=step * per), :]
            for row in (j,) if j < 8 else (8, 15):
                if whose == 0:
                    steps[pl.ds(base + row, 8, stride=16), :] = value
                else:
                    steps[pl.ds(base + 6 * 16 + row, 2, stride=16), :] = value[:2]
                    steps[pl.ds(base + row, 6, stride=16), :] = value[2:]

    def moved(value, move, sense):
        if move == 0:
            return value
        if sense > 0:
            here = pltpu.roll(value, SIDE - move, 1)
            return jnp.where(lane < SIDE - move, here, pltpu.roll(here, 15, 0))
        here = pltpu.roll(value, move, 1)
        return jnp.where(lane >= move, here, pltpu.roll(here, 1, 0))

    for which, sense in enumerate((1, -1)):
        level = [[steps[pl.ds(16 * s, 16), :]] for s in range(NT)]
        length = 1
        while len(level) > 1:
            level = [
                [
                    level[j][d // 2] + moved(level[j + 1][d // 2], d - d // 2, sense)
                    for d in range(2 * length)
                ]
                for j in range(0, len(level), 2)
            ]
            length *= 2
        for d in range(NT):
            flat[pl.ds(8 * d, 8), :] = level[0][d][:8]
        for r in range(8):
            out_ref[which, :, pl.ds(r * SIDE, SIDE)] = flat[pl.ds(r, NT, stride=8), :] * scale


def call(body, name, args, shape, dtype, scratch, flops=1 << 20, after=(), specs=None, params=PARAMS):
    def ordered(*refs):
        body(*refs[: len(args)], *refs[len(args) + len(after) :])

    return pl.pallas_call(
        ordered,
        in_specs=(specs or [VMEM] * len(args)) + [ANY] * len(after),
        out_specs=VMEM,
        out_shape=jax.ShapeDtypeStruct(shape, dtype),
        scratch_shapes=scratch,
        compiler_params=params,
        cost_estimate=pl.CostEstimate(flops=flops, bytes_accessed=1 << 20, transcendentals=0),
        name=name,
    )(*args, *after)


def bind(body, *first):
    def bound(*refs):
        body(*first, *refs)

    return bound


def per_device(voltages, taps):
    channels, _, _, frames, length = voltages.shape
    count = taps.shape[0]
    peers = lax.axis_size("tm")
    f32, bf16 = jnp.float32, jnp.bfloat16
    fourier, cos, sin = tables(SIDE)
    back = jnp.asarray(np.ascontiguousarray(fourier.T))
    fourier, cos, sin = jnp.asarray(fourier), jnp.asarray(cos), jnp.asarray(sin)
    rows = voltages.reshape(channels, 2, 2, frames, SIDE, SIDE).transpose(0, 1, 2, 4, 3, 5)
    rows = rows.reshape(channels, 2, 2, SIDE * frames, SIDE)
    coefficients = taps.reshape(count, SIDE, SIDE).transpose(1, 0, 2).reshape(SIDE * count, SIDE)
    pairs = [(i, i + 1) for i in range(2 * peers - 1)]
    tile = (SIDE, SIDE)

    halo = (2, 2, count - 1, SIDE, SIDE)
    interleaved = (SIDE * frames, SIDE)
    first = call(
        first_pack_kernel,
        "pack_first",
        [rows],
        halo,
        bf16,
        [
            pltpu.VMEM((2, 2) + interleaved, bf16),
            pltpu.VMEM((2, 2) + interleaved, f32),
            pltpu.SemaphoreType.DMA((2, 2)),
        ],
        specs=[ANY],
        params=FIRST,
    )
    packs = [first]
    near = [lax.ppermute(first, ("half", "tm"), pairs)]

    def send(place, pols, after):
        shape = (len(pols),) + halo[1:]
        body = bind(pack_kernel, place, pols)
        value = call(body, "pack", [rows], shape, bf16, [pltpu.VMEM((2,) + interleaved, f32)], after=after)
        packs.append(value)
        near.append(lax.ppermute(value, ("half", "tm"), pairs))

    constants = [coefficients, fourier, back, cos, sin]
    scratch = [
        pltpu.VMEM((2,) + interleaved, f32),
        pltpu.VMEM((2 * SIDE, frames * SIDE), bf16),
        pltpu.VMEM((frames * SIDE, 2 * SIDE), bf16),
    ]
    flops = 300 << 20
    for place in range(1, AHEAD):
        send(place, (0, 1), [first])
    plane = 2 * peers // channels
    shipped = (16 + channels // 2 * SIDE + 16, SIDE)
    across, edge = [], (channels // 2 - 1) * plane + plane - 1
    for i in range(2 * peers):
        half, at = divmod(i, peers)
        across.append((i, (1 - half) * peers + (at + plane) % peers))
    straight = [pair for pair in across if pair[0] != edge]
    target = dict(across)[edge]
    beside = edge - 4
    power = []
    last = channels - 1
    for place in range(last):
        args = [rows, near[place], *constants]
        order = power[-1:] + ([theirs, by] if place == last - 2 else [])
        power.append(call(bind(chunk_kernel, place), "chunk", args, tile, f32, scratch, flops, after=order))
        if place == channels // 2:
            ship = call(ship_kernel, "ship", power[:5], shipped, bf16, [], after=[packs[-1]])
            theirs = lax.ppermute(ship, ("half", "tm"), straight)
            by = lax.ppermute(ship, ("half", "tm"), [(edge, beside)])
            relayed = lax.ppermute(by, ("half", "tm"), [(beside, target)])
        if place + AHEAD < last:
            send(place + AHEAD, (0, 1), power[-1:])
        elif place + AHEAD == last:
            send(last, (0,), power[-1:])
            send(last, (1,), power[-1:])
    args = [rows, near[last], *constants]
    part = call(bind(first_half_kernel, last), "chunk_half", args, tile, f32, scratch, flops // 2, after=power[-1:])
    every = pltpu.VMEM((8 + 4 * SIDE + 8, SIDE), f32)
    sent = (2 * peers * SENT, SIDE)
    out = call(
        bind(last_kernel, last),
        "last",
        [rows, near[last + 1], *constants, part, power[0], power[3], power[4], power[5], power[6], theirs, relayed],
        sent,
        bf16,
        scratch + [every, pltpu.VMEM(sent, f32), pltpu.VMEM(shipped, f32)],
        flops // 2,
    )
    out = out.reshape(peers, SENT, 2, SIDE)
    owned = lax.all_to_all(out, "tm", split_axis=0, concat_axis=0, tiled=True).reshape(sent)
    scale = 1.0 / (frames * 2 * peers)
    return call(
        bind(tree_kernel, scale),
        "tree",
        [owned],
        (2, NT, channels * length // (2 * peers)),
        f32,
        [pltpu.VMEM(sent, f32), pltpu.VMEM((16 * NT, SIDE), f32), pltpu.VMEM((8 * NT, SIDE), f32)],
    )


def solution(mesh):
    peers, groups = mesh.shape["tm"], mesh.shape["chan"]
    halves = Mesh(mesh.devices.reshape(2, peers // 2, groups), ("half", "tm", "chan"))
    split = ("half", "tm")
    placed = (P("chan", None, None, split, None), P())
    return jax.shard_map(per_device, mesh=halves, in_specs=placed, out_specs=P("chan", None, split), check_vma=False)
```

```python
import math

import jax
import jax.numpy as jnp
import ml_dtypes
import numpy as np
from jax import lax
from jax.experimental import pallas as pl
from jax.experimental.pallas import tpu as pltpu
from jax.sharding import Mesh
from jax.sharding import PartitionSpec as P

NT = 16
SIDE = 128
BLOCK = 16
AHEAD = 4
SENT = 9
PARAMS = pltpu.CompilerParams(vmem_limit_bytes=12 << 20)
FIRST = pltpu.CompilerParams(vmem_limit_bytes=56_000_000)
VMEM = pl.BlockSpec(memory_space=pltpu.VMEM)
ANY = pl.BlockSpec(memory_space=pl.ANY)


def tables(side):
    index = np.arange(side, dtype=np.int64)
    angle = -2.0 * math.pi / side * ((index[:, None] * index[None, :]) % side)
    re = (np.cos(angle) / math.sqrt(side)).astype(ml_dtypes.bfloat16)
    im = (np.sin(angle) / math.sqrt(side)).astype(ml_dtypes.bfloat16)
    fourier = np.block([[re, -im], [im, re]])
    turn = -2.0 * math.pi / (side * side) * (index[:, None] * index[None, :])
    return fourier, np.cos(turn).astype(np.float32), np.sin(turn).astype(np.float32)


def channel_at(place, half):
    lower = place + 4 if place < 4 else 3 if place == 4 else place - 5
    return lower + half * (place - lower)


def receiver_half():
    half, last = lax.axis_index("half"), lax.axis_size("tm") - 1
    return jnp.where((half == 0) & (lax.axis_index("tm") == last), 1, half)


def spread(value, rows, out_ref, p, r):
    frames = value.shape[0] // SIDE
    rows[...] = value.astype(jnp.float32)
    for t in range(1, frames):
        out_ref[p, r, t - 1] = rows[pl.ds(t, SIDE, stride=frames), :].astype(jnp.bfloat16)


def first_pack_kernel(v_ref, out_ref, block, rows, sems):
    channel = channel_at(0, receiver_half())
    copies = {}
    for p in range(2):
        for r in range(2):
            copies[p, r] = pltpu.make_async_copy(v_ref.at[channel, p, r], block.at[p, r], sems.at[p, r])
            copies[p, r].start()
    for p in range(2):
        for r in range(2):
            copies[p, r].wait()
            spread(block[p, r], rows.at[p, r], out_ref, p, r)


def pack_kernel(place, pols, v_ref, out_ref, rows):
    channel = channel_at(place, receiver_half())
    for i, p in enumerate(pols):
        for r in range(2):
            spread(v_ref[channel, p, r], rows.at[r], out_ref, i, r)


def filtered(ins, channel, p, halo, times, rows, put):
    v_ref, taps_ref = ins[:2]
    frames = v_ref.shape[3] // SIDE
    count = taps_ref.shape[0] // SIDE
    lane = lax.broadcasted_iota(jnp.int32, (BLOCK, SIDE), 1)
    sign = 1.0 - 2.0 * (lane % 2).astype(jnp.float32)
    for r in range(2):
        rows[r] = v_ref[channel, p, r].astype(jnp.float32)
    for n in range(0, SIDE, BLOCK):
        shaped = [taps_ref[pl.ds(count * n + k, BLOCK, stride=count), :] * sign for k in range(count)]
        for r in range(2):
            frame = {t: rows[r, pl.ds(frames * n + t, BLOCK, stride=frames), :] for t in range(max(times) + 1)}
            if halo is not None:
                for t in range(1 - count, 0):
                    frame[t] = halo[r, t + count - 1, pl.ds(n, BLOCK), :].astype(jnp.float32)
            for t in times:
                value = shaped[0] * frame[t]
                for k in range(1, count):
                    if t - k in frame:
                        value = value + shaped[k] * frame[t - k]
                put(r, n, t, value)


def into(wide, order):
    def put(r, n, t, value):
        wide[pl.ds(r * SIDE + n, BLOCK), pl.ds(order.index(t) * SIDE, SIDE)] = value.astype(jnp.bfloat16)

    return put


def power_of(ins, wide, tall, many):
    fourier_ref, back_ref, cos_ref, sin_ref = ins[2:]
    span = many * SIDE
    first = jnp.dot(fourier_ref[...], wide[:, pl.ds(0, span)], preferred_element_type=jnp.float32)
    cos, sin = cos_ref[...], sin_ref[...]
    for i in range(many):
        re = first[:SIDE, i * SIDE : (i + 1) * SIDE]
        im = first[SIDE:, i * SIDE : (i + 1) * SIDE]
        tall[pl.ds(i * SIDE, SIDE), pl.ds(0, SIDE)] = (re * cos - im * sin).astype(jnp.bfloat16)
        tall[pl.ds(i * SIDE, SIDE), pl.ds(SIDE, SIDE)] = (re * sin + im * cos).astype(jnp.bfloat16)
    spectrum = jnp.dot(tall[pl.ds(0, span), :], back_ref[...], preferred_element_type=jnp.float32)
    square = spectrum * spectrum
    total = None
    for i in range(many):
        part = square[i * SIDE : (i + 1) * SIDE]
        part = part[:, :SIDE] + part[:, SIDE:]
        total = part if total is None else total + part
    return total


def chunk_kernel(place, *refs):
    ins, near, out_ref, (rows, wide, tall) = refs[:6], refs[6], refs[7], refs[8:]
    channel = channel_at(place, lax.axis_index("half"))
    times = list(range(ins[0].shape[3] // SIDE))
    total = None
    for p in range(2):
        filtered(ins, channel, p, near.at[p], times, rows, into(wide, times))
        power = power_of(ins, wide, tall, len(times))
        total = power if total is None else total + power
    out_ref[...] = total.T


def early_kernel(place, *refs):
    ins, near, out_ref, sums_ref, (rows, wide, tall) = refs[:6], refs[6], refs[7], refs[8], refs[9:]
    channel = channel_at(place, lax.axis_index("half"))
    frames = ins[0].shape[3] // SIDE
    times = list(range(frames))
    filtered(ins, channel, 0, near.at[0], times, rows, into(wide, times))
    total = power_of(ins, wide, tall, frames)
    whole = into(wide, [frames - 1])

    def put(r, n, t, value):
        if t == frames - 1:
            whole(r, n, t, value)
        else:
            sums_ref[r, t, pl.ds(n, BLOCK), :] = value

    filtered(ins, channel, 1, None, times, rows, put)
    out_ref[...] = total + power_of(ins, wide, tall, 1)


def late_power(ins, late, sums_ref, wide, tall):
    taps_ref = ins[1]
    count = taps_ref.shape[0] // SIDE
    lane = lax.broadcasted_iota(jnp.int32, (BLOCK, SIDE), 1)
    sign = 1.0 - 2.0 * (lane % 2).astype(jnp.float32)
    put = into(wide, list(range(count - 1)))
    for n in range(0, SIDE, BLOCK):
        shaped = [taps_ref[pl.ds(count * n + k, BLOCK, stride=count), :] * sign for k in range(1, count)]
        for r in range(2):
            frame = [late[0, r, t, pl.ds(n, BLOCK), :].astype(jnp.float32) for t in range(count - 1)]
            for t in range(count - 1):
                value = sums_ref[r, t, pl.ds(n, BLOCK), :]
                for k in range(t + 1, count):
                    value = value + shaped[k - 1] * frame[t - k + count - 1]
                put(r, n, t, value)
    return power_of(ins, wide, tall, count - 1)


def lay_out(every, apart, peers, step, start):
    for j in range(8):
        apart[pl.ds(start + j, peers, stride=step), :] = every[pl.ds(8 + j, peers, stride=8), :]
    lane = lax.broadcasted_iota(jnp.int32, (peers, SIDE), 1)
    after = every[pl.ds(16, peers, stride=8), :]
    before = every[pl.ds(7, peers, stride=8), :]
    apart[pl.ds(start + 8, peers, stride=step), :] = jnp.where(lane < SIDE // 2, after, before)


def ends(every, before, after):
    count = every.shape[0]
    every[pl.ds(0, 8), :] = before
    every[pl.ds(count - 8, 8), :] = after


def ship_kernel(p0, p1, p2, p3, border, out_ref):
    half = lax.axis_index("half")
    zero = jnp.zeros((8, SIDE), jnp.float32)
    before = jnp.where(half == 0, border[pl.ds(SIDE - 8, 8), :], zero)
    after = jnp.where(half == 1, border[pl.ds(0, 8), :], zero)
    out_ref[pl.ds(0, 16), :] = jnp.concatenate([zero, before], axis=0).astype(jnp.bfloat16)
    for i, ref in enumerate((p0, p1, p2, p3)):
        out_ref[pl.ds(16 + i * SIDE, SIDE), :] = ref[...].astype(jnp.bfloat16)
    out_ref[pl.ds(16 + 4 * SIDE, 16), :] = jnp.concatenate([after, zero], axis=0).astype(jnp.bfloat16)


def lay_kernel(p0, p3, border, p5, p6, theirs, relayed, out_ref, every, plain):
    half = lax.axis_index("half")
    peers = out_ref.shape[0] // (2 * SENT)
    plain[...] = theirs[...].astype(jnp.float32) + relayed[...].astype(jnp.float32)
    lay_out(plain.at[pl.ds(8, plain.shape[0] - 16)], out_ref, peers, 2 * SENT, SENT)

    def put(slot, value):
        every[pl.ds(pl.multiple_of(8 + slot * SIDE, 8), SIDE), :] = value

    put(3 * (1 - half), border[...])
    put(half, p5[...])
    put(1 + half, p6[...])
    put(2 + half, jnp.zeros((SIDE, SIDE), jnp.float32))
    zero = jnp.zeros((8, SIDE), jnp.float32)
    ends(
        every,
        jnp.where(half == 1, p3[pl.ds(SIDE - 8, 8), :], zero),
        jnp.where(half == 0, p0[pl.ds(0, 8), :], zero),
    )
    lay_out(every, out_ref, peers, 2 * SENT, 0)


def last_kernel(*refs):
    ins, (late, part, sums_ref, border, p6, laid), out_ref, same_ref = refs[:6], refs[6:12], refs[12], refs[13]
    wide, tall, every = refs[14:]
    half = lax.axis_index("half")
    value = (part[...] + late_power(ins, late, sums_ref, wide, tall)).T
    every[pl.ds(8, SIDE), :] = value
    zero = jnp.zeros((8, SIDE), jnp.float32)
    ends(every, p6[pl.ds(SIDE - 8, 8), :], jnp.where(half == 0, border[pl.ds(0, 8), :], zero))
    group = SIDE // 8
    stride = 2 * SENT
    start = group * stride * (2 + half)
    lay_out(every, same_ref, group, stride, start)
    lane = lax.broadcasted_iota(jnp.int32, (1, SIDE), 1)
    row = pl.ds(start - stride + 8, 1)
    same_ref[row, :] = jnp.where(lane < SIDE // 2, value[:1], same_ref[row, :])

    @pl.when(half == 0)
    def _():
        row = pl.ds(3 * group * stride + 8, 1)
        same_ref[row, :] = jnp.where(lane < SIDE // 2, same_ref[row, :], value[SIDE - 1 :])

    out_ref[...] = same_ref[...].astype(jnp.bfloat16)


def tree_kernel(scale, in_ref, out_ref, wide, steps, flat):
    half = lax.axis_index("half")
    step = 2 * SENT
    sources = in_ref.shape[0] // step
    per = sources // (NT // 2)
    lane = lax.broadcasted_iota(jnp.int32, (16, SIDE), 1)
    wide[...] = in_ref[...].astype(jnp.float32)
    steps[...] = jnp.zeros(steps.shape, jnp.float32)
    for whose in range(2):
        base = 8 * 16 * (half if whose == 0 else 1 - half)
        for j in range(SENT):
            value = wide[pl.ds(whose * SENT + j, 8, stride=step * per), :]
            for i in range(1, per):
                value = value + wide[pl.ds(step * i + whose * SENT + j, 8, stride=step * per), :]
            for row in (j,) if j < 8 else (8, 15):
                if whose == 0:
                    steps[pl.ds(base + row, 8, stride=16), :] = value
                else:
                    steps[pl.ds(base + 6 * 16 + row, 2, stride=16), :] = value[:2]
                    steps[pl.ds(base + row, 6, stride=16), :] = value[2:]

    def moved(value, move, sense):
        if move == 0:
            return value
        if sense > 0:
            here = pltpu.roll(value, SIDE - move, 1)
            return jnp.where(lane < SIDE - move, here, pltpu.roll(here, 15, 0))
        here = pltpu.roll(value, move, 1)
        return jnp.where(lane >= move, here, pltpu.roll(here, 1, 0))

    for which, sense in enumerate((1, -1)):
        level = [[steps[pl.ds(16 * s, 16), :]] for s in range(NT)]
        length = 1
        while len(level) > 1:
            level = [
                [
                    level[j][d // 2] + moved(level[j + 1][d // 2], d - d // 2, sense)
                    for d in range(2 * length)
                ]
                for j in range(0, len(level), 2)
            ]
            length *= 2
        for d in range(NT):
            flat[pl.ds(8 * d, 8), :] = level[0][d][:8]
        for r in range(8):
            out_ref[which, :, pl.ds(r * SIDE, SIDE)] = flat[pl.ds(r, NT, stride=8), :] * scale


def call(body, name, args, shape, dtype, scratch, flops=1 << 20, after=(), specs=None, params=PARAMS, alias=None):
    several = isinstance(shape, list)

    def ordered(*refs):
        body(*refs[: len(args)], *refs[len(args) + len(after) :])

    return pl.pallas_call(
        ordered,
        in_specs=(specs or [VMEM] * len(args)) + [ANY] * len(after),
        out_specs=[VMEM] * len(shape) if several else VMEM,
        out_shape=[jax.ShapeDtypeStruct(*each) for each in shape] if several else jax.ShapeDtypeStruct(shape, dtype),
        scratch_shapes=scratch,
        input_output_aliases=alias or {},
        compiler_params=params,
        cost_estimate=pl.CostEstimate(flops=flops, bytes_accessed=1 << 20, transcendentals=0),
        name=name,
    )(*args, *after)


def bind(body, *first):
    def bound(*refs):
        body(*first, *refs)

    return bound


def per_device(voltages, taps):
    channels, _, _, frames, length = voltages.shape
    count = taps.shape[0]
    peers = lax.axis_size("tm")
    f32, bf16 = jnp.float32, jnp.bfloat16
    fourier, cos, sin = tables(SIDE)
    back = jnp.asarray(np.ascontiguousarray(fourier.T))
    fourier, cos, sin = jnp.asarray(fourier), jnp.asarray(cos), jnp.asarray(sin)
    rows = voltages.reshape(channels, 2, 2, frames, SIDE, SIDE).transpose(0, 1, 2, 4, 3, 5)
    rows = rows.reshape(channels, 2, 2, SIDE * frames, SIDE)
    coefficients = taps.reshape(count, SIDE, SIDE).transpose(1, 0, 2).reshape(SIDE * count, SIDE)
    pairs = [(i, i + 1) for i in range(2 * peers - 1)]
    tile = (SIDE, SIDE)

    halo = (2, 2, count - 1, SIDE, SIDE)
    interleaved = (SIDE * frames, SIDE)
    first = call(
        first_pack_kernel,
        "pack_first",
        [rows],
        halo,
        bf16,
        [
            pltpu.VMEM((2, 2) + interleaved, bf16),
            pltpu.VMEM((2, 2) + interleaved, f32),
            pltpu.SemaphoreType.DMA((2, 2)),
        ],
        specs=[ANY],
        params=FIRST,
    )
    packs = [first]
    near = [[lax.ppermute(first, ("half", "tm"), pairs)]] + [[] for _ in range(channels - 1)]

    def send(place, pols, after):
        shape = (len(pols),) + halo[1:]
        body = bind(pack_kernel, place, pols)
        value = call(body, "pack", [rows], shape, bf16, [pltpu.VMEM((2,) + interleaved, f32)], after=after)
        packs.append(value)
        near[place].append(lax.ppermute(value, ("half", "tm"), pairs))

    constants = [coefficients, fourier, back, cos, sin]
    scratch = [
        pltpu.VMEM((2,) + interleaved, f32),
        pltpu.VMEM((2 * SIDE, frames * SIDE), bf16),
        pltpu.VMEM((frames * SIDE, 2 * SIDE), bf16),
    ]
    flops = 300 << 20
    for place in range(1, AHEAD):
        send(place, (0, 1), [first])
    plane = 2 * peers // channels
    shipped = (16 + channels // 2 * SIDE + 16, SIDE)
    across, edge = [], (channels // 2 - 1) * plane + plane - 1
    for i in range(2 * peers):
        half, at = divmod(i, peers)
        across.append((i, (1 - half) * peers + (at + plane) % peers))
    straight = [pair for pair in across if pair[0] != edge]
    target = dict(across)[edge]
    beside = edge - 4
    power = []
    last = channels - 1
    for place in range(last):
        args = [rows, *constants, *near[place]]
        order = power[-1:] + ([theirs, by] if place == last - 2 else [])
        body = bind(chunk_kernel, place)
        power.append(call(body, "chunk", args, tile, f32, scratch, flops, after=order))
        if place == channels // 2:
            ship = call(ship_kernel, "ship", power[:5], shipped, bf16, [], after=[packs[-1]])
            theirs = lax.ppermute(ship, ("half", "tm"), straight)
            by = lax.ppermute(ship, ("half", "tm"), [(edge, beside)])
            relayed = lax.ppermute(by, ("half", "tm"), [(beside, target)])
        if place + AHEAD < last:
            send(place + AHEAD, (0, 1), power[-1:])
        elif place + AHEAD == last:
            send(last, (0,), power[-1:])
            send(last, (1,), power[-1:])
    sums = (2, count - 1) + tile
    part, begun = call(
        bind(early_kernel, last),
        "chunk_early",
        [rows, *constants, near[last][0]],
        [(tile, f32), (sums, f32)],
        None,
        scratch,
        flops,
        after=power[-1:],
    )
    sent = (2 * peers * SENT, SIDE)
    laid = call(
        lay_kernel,
        "lay",
        [power[0], power[3], *power[4:7], theirs, relayed],
        sent,
        f32,
        [pltpu.VMEM((8 + 4 * SIDE + 8, SIDE), f32), pltpu.VMEM(shipped, f32)],
        after=[part],
    )
    out, _ = call(
        last_kernel,
        "last",
        [rows, *constants, near[last][1], part, begun, power[4], power[6], laid],
        [(sent, bf16), (sent, f32)],
        None,
        scratch[1:] + [pltpu.VMEM((8 + SIDE + 8, SIDE), f32)],
        flops // 2,
        alias={11: 1},
    )
    out = out.reshape(peers, SENT, 2, SIDE)
    owned = lax.all_to_all(out, "tm", split_axis=0, concat_axis=0, tiled=True).reshape(sent)
    scale = 1.0 / (frames * 2 * peers)
    return call(
        bind(tree_kernel, scale),
        "tree",
        [owned],
        (2, NT, channels * length // (2 * peers)),
        f32,
        [pltpu.VMEM(sent, f32), pltpu.VMEM((16 * NT, SIDE), f32), pltpu.VMEM((8 * NT, SIDE), f32)],
    )


def solution(mesh):
    peers, groups = mesh.shape["tm"], mesh.shape["chan"]
    halves = Mesh(mesh.devices.reshape(2, peers // 2, groups), ("half", "tm", "chan"))
    split = ("half", "tm")
    placed = (P("chan", None, None, split, None), P())
    return jax.shard_map(per_device, mesh=halves, in_specs=placed, out_specs=P("chan", None, split), check_vma=False)
```

```python
import math

import jax
import jax.numpy as jnp
import ml_dtypes
import numpy as np
from jax import lax
from jax.experimental import pallas as pl
from jax.experimental.pallas import tpu as pltpu
from jax.sharding import Mesh
from jax.sharding import PartitionSpec as P

NT = 16
SIDE = 128
BLOCK = 16
AHEAD = 4
SENT = 9
SPARE = 24
PARAMS = pltpu.CompilerParams(vmem_limit_bytes=12 << 20)
FIRST = pltpu.CompilerParams(vmem_limit_bytes=56_000_000)
VMEM = pl.BlockSpec(memory_space=pltpu.VMEM)
ANY = pl.BlockSpec(memory_space=pl.ANY)


def tables(side):
    index = np.arange(side, dtype=np.int64)
    angle = -2.0 * math.pi / side * ((index[:, None] * index[None, :]) % side)
    re = (np.cos(angle) / math.sqrt(side)).astype(ml_dtypes.bfloat16)
    im = (np.sin(angle) / math.sqrt(side)).astype(ml_dtypes.bfloat16)
    fourier = np.block([[re, -im], [im, re]])
    turn = -2.0 * math.pi / (side * side) * (index[:, None] * index[None, :])
    return fourier, np.cos(turn).astype(np.float32), np.sin(turn).astype(np.float32)


def channel_at(place, half):
    lower = place + 4 if place < 4 else 3 if place == 4 else place - 5
    return lower + half * (place - lower)


def receiver_half():
    half, last = lax.axis_index("half"), lax.axis_size("tm") - 1
    return jnp.where((half == 0) & (lax.axis_index("tm") == last), 1, half)


def spread(value, rows, out_ref, p, r):
    frames = value.shape[0] // SIDE
    rows[pl.ds(0, value.shape[0]), :] = value.astype(jnp.float32)
    for t in range(1, frames):
        out_ref[p, r, t - 1] = rows[pl.ds(t, SIDE, stride=frames), :].astype(jnp.bfloat16)


def first_pack_kernel(v_ref, out_ref, block, rows, sems):
    channel = channel_at(0, receiver_half())
    copies = {}
    for p in range(2):
        for r in range(2):
            copies[p, r] = pltpu.make_async_copy(v_ref.at[channel, p, r], block.at[p, r], sems.at[p, r])
            copies[p, r].start()
    for p in range(2):
        for r in range(2):
            copies[p, r].wait()
            spread(block[p, r], rows.at[p, r], out_ref, p, r)


def pack_kernel(place, pols, v_ref, out_ref, rows):
    channel = channel_at(place, receiver_half())
    for i, p in enumerate(pols):
        for r in range(2):
            spread(v_ref[channel, p, r], rows.at[r], out_ref, i, r)


def filtered(ins, channel, p, halo, times, rows, put):
    v_ref, taps_ref = ins[:2]
    frames = v_ref.shape[3] // SIDE
    count = taps_ref.shape[0] // SIDE
    lane = lax.broadcasted_iota(jnp.int32, (BLOCK, SIDE), 1)
    sign = 1.0 - 2.0 * (lane % 2).astype(jnp.float32)
    for r in range(2):
        rows[r, pl.ds(0, frames * SIDE), :] = v_ref[channel, p, r].astype(jnp.float32)
    for n in range(0, SIDE, BLOCK):
        shaped = [taps_ref[pl.ds(count * n + k, BLOCK, stride=count), :] * sign for k in range(count)]
        for r in range(2):
            frame = {t: rows[r, pl.ds(frames * n + t, BLOCK, stride=frames), :] for t in range(max(times) + 1)}
            if halo is not None:
                for t in range(1 - count, 0):
                    frame[t] = halo[r, t + count - 1, pl.ds(n, BLOCK), :].astype(jnp.float32)
            for t in times:
                value = shaped[0] * frame[t]
                for k in range(1, count):
                    if t - k in frame:
                        value = value + shaped[k] * frame[t - k]
                put(r, n, t, value)


def into(wide, order):
    def put(r, n, t, value):
        wide[pl.ds(r * SIDE + n, BLOCK), pl.ds(order.index(t) * SIDE, SIDE)] = value.astype(jnp.bfloat16)

    return put


def power_of(ins, wide, tall, many):
    fourier_ref, back_ref, cos_ref, sin_ref = ins[2:]
    span = many * SIDE
    first = jnp.dot(fourier_ref[...], wide[:, pl.ds(0, span)], preferred_element_type=jnp.float32)
    cos, sin = cos_ref[...], sin_ref[...]
    for i in range(many):
        re = first[:SIDE, i * SIDE : (i + 1) * SIDE]
        im = first[SIDE:, i * SIDE : (i + 1) * SIDE]
        tall[pl.ds(i * SIDE, SIDE), pl.ds(0, SIDE)] = (re * cos - im * sin).astype(jnp.bfloat16)
        tall[pl.ds(i * SIDE, SIDE), pl.ds(SIDE, SIDE)] = (re * sin + im * cos).astype(jnp.bfloat16)
    spectrum = jnp.dot(tall[pl.ds(0, span), :], back_ref[...], preferred_element_type=jnp.float32)
    square = spectrum * spectrum
    total = None
    for i in range(many):
        part = square[i * SIDE : (i + 1) * SIDE]
        part = part[:, :SIDE] + part[:, SIDE:]
        total = part if total is None else total + part
    return total


def chunk_kernel(place, *refs):
    ins, near, out_ref, (rows, wide, tall) = refs[:6], refs[6], refs[7], refs[8:]
    channel = channel_at(place, lax.axis_index("half"))
    times = list(range(ins[0].shape[3] // SIDE))
    total = None
    for p in range(2):
        filtered(ins, channel, p, near.at[p], times, rows, into(wide, times))
        power = power_of(ins, wide, tall, len(times))
        total = power if total is None else total + power
    out_ref[...] = total.T


def early_kernel(place, *refs):
    ins, near, out_ref, sums_ref, (rows, wide, tall) = refs[:6], refs[6], refs[7], refs[8], refs[9:]
    channel = channel_at(place, lax.axis_index("half"))
    frames = ins[0].shape[3] // SIDE
    times = list(range(frames))
    filtered(ins, channel, 0, near.at[0], times, rows, into(wide, times))
    total = power_of(ins, wide, tall, frames)
    whole = into(wide, [frames - 1])

    def put(r, n, t, value):
        if t == frames - 1:
            whole(r, n, t, value)
        else:
            sums_ref[r, t, pl.ds(n, BLOCK), :] = value

    filtered(ins, channel, 1, None, times, rows, put)
    out_ref[...] = total + power_of(ins, wide, tall, 1)


def late_power(ins, late, sums_ref, wide, tall):
    taps_ref = ins[1]
    count = taps_ref.shape[0] // SIDE
    lane = lax.broadcasted_iota(jnp.int32, (BLOCK, SIDE), 1)
    sign = 1.0 - 2.0 * (lane % 2).astype(jnp.float32)
    put = into(wide, list(range(count - 1)))
    for n in range(0, SIDE, BLOCK):
        shaped = [taps_ref[pl.ds(count * n + k, BLOCK, stride=count), :] * sign for k in range(1, count)]
        for r in range(2):
            frame = [late[0, r, t, pl.ds(n, BLOCK), :].astype(jnp.float32) for t in range(count - 1)]
            for t in range(count - 1):
                value = sums_ref[r, t, pl.ds(n, BLOCK), :]
                for k in range(t + 1, count):
                    value = value + shaped[k - 1] * frame[t - k + count - 1]
                put(r, n, t, value)
    return power_of(ins, wide, tall, count - 1)


def lay_out(every, apart, peers, step, start):
    for j in range(8):
        apart[pl.ds(start + j, peers, stride=step), :] = every[pl.ds(8 + j, peers, stride=8), :]
    lane = lax.broadcasted_iota(jnp.int32, (peers, SIDE), 1)
    after = every[pl.ds(16, peers, stride=8), :]
    before = every[pl.ds(7, peers, stride=8), :]
    apart[pl.ds(start + 8, peers, stride=step), :] = jnp.where(lane < SIDE // 2, after, before)


def ends(every, before, after):
    count = every.shape[0]
    every[pl.ds(0, 8), :] = before
    every[pl.ds(count - 8, 8), :] = after


def ship_kernel(p0, p1, p2, p3, border, out_ref):
    half = lax.axis_index("half")
    zero = jnp.zeros((8, SIDE), jnp.float32)
    before = jnp.where(half == 0, border[pl.ds(SIDE - 8, 8), :], zero)
    after = jnp.where(half == 1, border[pl.ds(0, 8), :], zero)
    out_ref[pl.ds(0, 16), :] = jnp.concatenate([zero, before], axis=0).astype(jnp.bfloat16)
    for i, ref in enumerate((p0, p1, p2, p3)):
        out_ref[pl.ds(16 + i * SIDE, SIDE), :] = ref[...].astype(jnp.bfloat16)
    out_ref[pl.ds(16 + 4 * SIDE, 16), :] = jnp.concatenate([after, zero], axis=0).astype(jnp.bfloat16)


def lay_kernel(p0, p3, border, p5, p6, theirs, relayed, out_ref, every, plain):
    half = lax.axis_index("half")
    peers = (out_ref.shape[0] - SPARE) // (2 * SENT)
    plain[...] = theirs[...].astype(jnp.float32) + relayed[...].astype(jnp.float32)
    lay_out(plain.at[pl.ds(8, plain.shape[0] - 16)], out_ref, peers, 2 * SENT, SENT)

    def put(slot, value):
        every[pl.ds(pl.multiple_of(8 + slot * SIDE, 8), SIDE), :] = value

    put(3 * (1 - half), border[...])
    put(half, p5[...])
    put(1 + half, p6[...])
    put(2 + half, jnp.zeros((SIDE, SIDE), jnp.float32))
    zero = jnp.zeros((8, SIDE), jnp.float32)
    ends(
        every,
        jnp.where(half == 1, p3[pl.ds(SIDE - 8, 8), :], zero),
        jnp.where(half == 0, p0[pl.ds(0, 8), :], zero),
    )
    lay_out(every, out_ref, peers, 2 * SENT, 0)


def last_kernel(*refs):
    ins, (late, part, sums_ref, border, p6, laid), out_ref, same_ref = refs[:6], refs[6:12], refs[12], refs[13]
    wide, tall, every = refs[14:]
    half = lax.axis_index("half")
    value = (part[...] + late_power(ins, late, sums_ref, wide, tall)).T
    every[pl.ds(8, SIDE), :] = value
    zero = jnp.zeros((8, SIDE), jnp.float32)
    ends(every, p6[pl.ds(SIDE - 8, 8), :], jnp.where(half == 0, border[pl.ds(0, 8), :], zero))
    group = SIDE // 8
    stride = 2 * SENT
    start = group * stride * (2 + half)
    lay_out(every, same_ref, group, stride, start)
    lane = lax.broadcasted_iota(jnp.int32, (1, SIDE), 1)
    row = pl.ds(start - stride + 8, 1)
    same_ref[row, :] = jnp.where(lane < SIDE // 2, value[:1], same_ref[row, :])

    @pl.when(half == 0)
    def _():
        row = pl.ds(3 * group * stride + 8, 1)
        same_ref[row, :] = jnp.where(lane < SIDE // 2, same_ref[row, :], value[SIDE - 1 :])

    out_ref[...] = same_ref[pl.ds(0, out_ref.shape[0]), :].astype(jnp.bfloat16)


def tree_kernel(scale, in_ref, out_ref, wide, steps, flat):
    half = lax.axis_index("half")
    step = 2 * SENT
    sources = in_ref.shape[0] // step
    per = sources // (NT // 2)
    lane = lax.broadcasted_iota(jnp.int32, (16, SIDE), 1)
    wide[pl.ds(0, in_ref.shape[0]), :] = in_ref[...].astype(jnp.float32)
    steps[...] = jnp.zeros(steps.shape, jnp.float32)
    for whose in range(2):
        base = 8 * 16 * (half if whose == 0 else 1 - half)
        for j in range(SENT):
            value = wide[pl.ds(whose * SENT + j, 8, stride=step * per), :]
            for i in range(1, per):
                value = value + wide[pl.ds(step * i + whose * SENT + j, 8, stride=step * per), :]
            for row in (j,) if j < 8 else (8, 15):
                if whose == 0:
                    steps[pl.ds(base + row, 8, stride=16), :] = value
                else:
                    steps[pl.ds(base + 6 * 16 + row, 2, stride=16), :] = value[:2]
                    steps[pl.ds(base + row, 6, stride=16), :] = value[2:]

    def moved(value, move, sense):
        if move == 0:
            return value
        if sense > 0:
            here = pltpu.roll(value, SIDE - move, 1)
            return jnp.where(lane < SIDE - move, here, pltpu.roll(here, 15, 0))
        here = pltpu.roll(value, move, 1)
        return jnp.where(lane >= move, here, pltpu.roll(here, 1, 0))

    for which, sense in enumerate((1, -1)):
        level = [[steps[pl.ds(16 * s, 16), :]] for s in range(NT)]
        length = 1
        while len(level) > 1:
            level = [
                [
                    level[j][d // 2] + moved(level[j + 1][d // 2], d - d // 2, sense)
                    for d in range(2 * length)
                ]
                for j in range(0, len(level), 2)
            ]
            length *= 2
        for d in range(NT):
            flat[pl.ds(8 * d, 8), :] = level[0][d][:8]
        for r in range(8):
            out_ref[which, :, pl.ds(r * SIDE, SIDE)] = flat[pl.ds(r, NT, stride=8), :] * scale


def call(body, name, args, shape, dtype, scratch, flops=1 << 20, after=(), specs=None, params=PARAMS, alias=None):
    several = isinstance(shape, list)

    def ordered(*refs):
        body(*refs[: len(args)], *refs[len(args) + len(after) :])

    return pl.pallas_call(
        ordered,
        in_specs=(specs or [VMEM] * len(args)) + [ANY] * len(after),
        out_specs=[VMEM] * len(shape) if several else VMEM,
        out_shape=[jax.ShapeDtypeStruct(*each) for each in shape] if several else jax.ShapeDtypeStruct(shape, dtype),
        scratch_shapes=scratch,
        input_output_aliases=alias or {},
        compiler_params=params,
        cost_estimate=pl.CostEstimate(flops=flops, bytes_accessed=1 << 20, transcendentals=0),
        name=name,
    )(*args, *after)


def bind(body, *first):
    def bound(*refs):
        body(*first, *refs)

    return bound


def per_device(voltages, taps):
    channels, _, _, frames, length = voltages.shape
    count = taps.shape[0]
    peers = lax.axis_size("tm")
    f32, bf16 = jnp.float32, jnp.bfloat16
    fourier, cos, sin = tables(SIDE)
    back = jnp.asarray(np.ascontiguousarray(fourier.T))
    fourier, cos, sin = jnp.asarray(fourier), jnp.asarray(cos), jnp.asarray(sin)
    rows = voltages.reshape(channels, 2, 2, frames, SIDE, SIDE).transpose(0, 1, 2, 4, 3, 5)
    rows = rows.reshape(channels, 2, 2, SIDE * frames, SIDE)
    coefficients = taps.reshape(count, SIDE, SIDE).transpose(1, 0, 2).reshape(SIDE * count, SIDE)
    pairs = [(i, i + 1) for i in range(2 * peers - 1)]
    tile = (SIDE, SIDE)

    halo = (2, 2, count - 1, SIDE, SIDE)
    interleaved = (SIDE * frames, SIDE)
    roomy = (SIDE * frames + 8, SIDE)
    first = call(
        first_pack_kernel,
        "pack_first",
        [rows],
        halo,
        bf16,
        [
            pltpu.VMEM((2, 2) + interleaved, bf16),
            pltpu.VMEM((2, 2) + roomy, f32),
            pltpu.SemaphoreType.DMA((2, 2)),
        ],
        specs=[ANY],
        params=FIRST,
    )
    packs = [first]
    near = [[lax.ppermute(first, ("half", "tm"), pairs)]] + [[] for _ in range(channels - 1)]

    def send(place, pols, after):
        shape = (len(pols),) + halo[1:]
        body = bind(pack_kernel, place, pols)
        value = call(body, "pack", [rows], shape, bf16, [pltpu.VMEM((2,) + roomy, f32)], after=after)
        packs.append(value)
        near[place].append(lax.ppermute(value, ("half", "tm"), pairs))

    constants = [coefficients, fourier, back, cos, sin]
    scratch = [
        pltpu.VMEM((2,) + roomy, f32),
        pltpu.VMEM((2 * SIDE, frames * SIDE), bf16),
        pltpu.VMEM((frames * SIDE, 2 * SIDE), bf16),
    ]
    flops = 300 << 20
    for place in range(1, AHEAD):
        send(place, (0, 1), [first])
    plane = 2 * peers // channels
    shipped = (16 + channels // 2 * SIDE + 16, SIDE)
    across, edge = [], (channels // 2 - 1) * plane + plane - 1
    for i in range(2 * peers):
        half, at = divmod(i, peers)
        across.append((i, (1 - half) * peers + (at + plane) % peers))
    straight = [pair for pair in across if pair[0] != edge]
    target = dict(across)[edge]
    beside = edge - 4
    power = []
    last = channels - 1
    for place in range(last):
        args = [rows, *constants, *near[place]]
        order = power[-1:] + ([theirs, by] if place == last - 2 else [])
        body = bind(chunk_kernel, place)
        power.append(call(body, "chunk", args, tile, f32, scratch, flops, after=order))
        if place == channels // 2:
            ship = call(ship_kernel, "ship", power[:5], shipped, bf16, [], after=[packs[-1]])
            theirs = lax.ppermute(ship, ("half", "tm"), straight)
            by = lax.ppermute(ship, ("half", "tm"), [(edge, beside)])
            relayed = lax.ppermute(by, ("half", "tm"), [(beside, target)])
        if place + AHEAD < last:
            send(place + AHEAD, (0, 1), power[-1:])
        elif place + AHEAD == last:
            send(last, (0,), power[-1:])
            send(last, (1,), power[-1:])
    sums = (2, count - 1) + tile
    part, begun = call(
        bind(early_kernel, last),
        "chunk_early",
        [rows, *constants, near[last][0]],
        [(tile, f32), (sums, f32)],
        None,
        scratch,
        flops,
        after=power[-1:],
    )
    sent = (2 * peers * SENT, SIDE)
    laid = call(
        lay_kernel,
        "lay",
        [power[0], power[3], *power[4:7], theirs, relayed],
        (sent[0] + SPARE, SIDE),
        f32,
        [pltpu.VMEM((8 + 4 * SIDE + 8, SIDE), f32), pltpu.VMEM(shipped, f32)],
        after=[part],
    )
    out, _ = call(
        last_kernel,
        "last",
        [rows, *constants, near[last][1], part, begun, power[4], power[6], laid],
        [(sent, bf16), ((sent[0] + SPARE, SIDE), f32)],
        None,
        scratch[1:] + [pltpu.VMEM((8 + SIDE + 8, SIDE), f32)],
        flops // 2,
        alias={11: 1},
    )
    out = out.reshape(peers, SENT, 2, SIDE)
    owned = lax.all_to_all(out, "tm", split_axis=0, concat_axis=0, tiled=True).reshape(sent)
    scale = 1.0 / (frames * 2 * peers)
    return call(
        bind(tree_kernel, scale),
        "tree",
        [owned],
        (2, NT, channels * length // (2 * peers)),
        f32,
        [
            pltpu.VMEM((sent[0] + 16 * SENT, SIDE), f32),
            pltpu.VMEM((16 * NT + 16, SIDE), f32),
            pltpu.VMEM((8 * NT + 8, SIDE), f32),
        ],
    )


def solution(mesh):
    peers, groups = mesh.shape["tm"], mesh.shape["chan"]
    halves = Mesh(mesh.devices.reshape(2, peers // 2, groups), ("half", "tm", "chan"))
    split = ("half", "tm")
    placed = (P("chan", None, None, split, None), P())
    return jax.shard_map(per_device, mesh=halves, in_specs=placed, out_specs=P("chan", None, split), check_vma=False)
```

```python
import math

import jax
import jax.numpy as jnp
import ml_dtypes
import numpy as np
from jax import lax
from jax.experimental import pallas as pl
from jax.experimental.pallas import tpu as pltpu
from jax.sharding import Mesh
from jax.sharding import PartitionSpec as P

NT = 16
SIDE = 128
BLOCK = 16
AHEAD = 4
SENT = 9
SPARE = 24
ROOM = 24
PARAMS = pltpu.CompilerParams(vmem_limit_bytes=12 << 20)
FIRST = pltpu.CompilerParams(vmem_limit_bytes=56_000_000)
VMEM = pl.BlockSpec(memory_space=pltpu.VMEM)
ANY = pl.BlockSpec(memory_space=pl.ANY)


def tables(side):
    index = np.arange(side, dtype=np.int64)
    angle = -2.0 * math.pi / side * ((index[:, None] * index[None, :]) % side)
    re = (np.cos(angle) / math.sqrt(side)).astype(ml_dtypes.bfloat16)
    im = (np.sin(angle) / math.sqrt(side)).astype(ml_dtypes.bfloat16)
    fourier = np.block([[re, -im], [im, re]])
    turn = -2.0 * math.pi / (side * side) * (index[:, None] * index[None, :])
    return fourier, np.cos(turn).astype(np.float32), np.sin(turn).astype(np.float32)


def channel_at(place, half):
    lower = place + 4 if place < 4 else 3 if place == 4 else place - 5
    return lower + half * (place - lower)


def receiver_half():
    half, last = lax.axis_index("half"), lax.axis_size("tm") - 1
    return jnp.where((half == 0) & (lax.axis_index("tm") == last), 1, half)


def spread(value, rows, out_ref, p, r):
    frames = value.shape[0] // SIDE
    rows[pl.ds(0, value.shape[0]), :] = value.astype(jnp.float32)
    for t in range(1, frames):
        out_ref[p, r, t - 1] = rows[pl.ds(t, SIDE, stride=frames), :].astype(jnp.bfloat16)


def first_pack_kernel(v_ref, out_ref, block, rows, sems):
    channel = channel_at(0, receiver_half())
    copies = {}
    for p in range(2):
        for r in range(2):
            copies[p, r] = pltpu.make_async_copy(v_ref.at[channel, p, r], block.at[p, r], sems.at[p, r])
            copies[p, r].start()
    for p in range(2):
        for r in range(2):
            copies[p, r].wait()
            spread(block[p, r], rows.at[p, r], out_ref, p, r)


def pack_kernel(place, pols, v_ref, out_ref, rows):
    channel = channel_at(place, receiver_half())
    for i, p in enumerate(pols):
        for r in range(2):
            spread(v_ref[channel, p, r], rows.at[r], out_ref, i, r)


def filtered(ins, channel, p, halo, times, rows, put):
    v_ref, taps_ref = ins[:2]
    frames = v_ref.shape[3] // SIDE
    count = taps_ref.shape[0] // SIDE
    lane = lax.broadcasted_iota(jnp.int32, (BLOCK, SIDE), 1)
    sign = 1.0 - 2.0 * (lane % 2).astype(jnp.float32)
    for r in range(2):
        rows[r, pl.ds(0, frames * SIDE), :] = v_ref[channel, p, r].astype(jnp.float32)
    for n in range(0, SIDE, BLOCK):
        shaped = [taps_ref[pl.ds(count * n + k, BLOCK, stride=count), :] * sign for k in range(count)]
        for r in range(2):
            frame = {t: rows[r, pl.ds(frames * n + t, BLOCK, stride=frames), :] for t in range(max(times) + 1)}
            if halo is not None:
                for t in range(1 - count, 0):
                    frame[t] = halo[r, t + count - 1, pl.ds(n, BLOCK), :].astype(jnp.float32)
            for t in times:
                value = shaped[0] * frame[t]
                for k in range(1, count):
                    if t - k in frame:
                        value = value + shaped[k] * frame[t - k]
                put(r, n, t, value)


def into(wide, order):
    def put(r, n, t, value):
        wide[pl.ds(r * SIDE + n, BLOCK), pl.ds(order.index(t) * SIDE, SIDE)] = value.astype(jnp.bfloat16)

    return put


def power_of(ins, wide, tall, many):
    fourier_ref, back_ref, cos_ref, sin_ref = ins[2:]
    span = many * SIDE
    first = jnp.dot(fourier_ref[...], wide[:, pl.ds(0, span)], preferred_element_type=jnp.float32)
    cos, sin = cos_ref[...], sin_ref[...]
    for i in range(many):
        re = first[:SIDE, i * SIDE : (i + 1) * SIDE]
        im = first[SIDE:, i * SIDE : (i + 1) * SIDE]
        tall[pl.ds(i * SIDE, SIDE), pl.ds(0, SIDE)] = (re * cos - im * sin).astype(jnp.bfloat16)
        tall[pl.ds(i * SIDE, SIDE), pl.ds(SIDE, SIDE)] = (re * sin + im * cos).astype(jnp.bfloat16)
    spectrum = jnp.dot(tall[pl.ds(0, span), :], back_ref[...], preferred_element_type=jnp.float32)
    square = spectrum * spectrum
    total = None
    for i in range(many):
        part = square[i * SIDE : (i + 1) * SIDE]
        part = part[:, :SIDE] + part[:, SIDE:]
        total = part if total is None else total + part
    return total


def chunk_kernel(place, *refs):
    ins, near, out_ref, (rows, wide, tall) = refs[:6], refs[6], refs[7], refs[8:]
    channel = channel_at(place, lax.axis_index("half"))
    times = list(range(ins[0].shape[3] // SIDE))
    total = None
    for p in range(2):
        filtered(ins, channel, p, near.at[p], times, rows, into(wide, times))
        power = power_of(ins, wide, tall, len(times))
        total = power if total is None else total + power
    out_ref[...] = total.T


def early_kernel(place, *refs):
    ins, near, out_ref, sums_ref, (rows, wide, tall) = refs[:6], refs[6], refs[7], refs[8], refs[9:]
    channel = channel_at(place, lax.axis_index("half"))
    frames = ins[0].shape[3] // SIDE
    times = list(range(frames))
    filtered(ins, channel, 0, near.at[0], times, rows, into(wide, times))
    total = power_of(ins, wide, tall, frames)
    whole = into(wide, [frames - 1])

    def put(r, n, t, value):
        if t == frames - 1:
            whole(r, n, t, value)
        else:
            sums_ref[r, t, pl.ds(n, BLOCK), :] = value

    filtered(ins, channel, 1, None, times, rows, put)
    out_ref[...] = total + power_of(ins, wide, tall, 1)


def late_power(ins, late, sums_ref, wide, tall):
    taps_ref = ins[1]
    count = taps_ref.shape[0] // SIDE
    lane = lax.broadcasted_iota(jnp.int32, (BLOCK, SIDE), 1)
    sign = 1.0 - 2.0 * (lane % 2).astype(jnp.float32)
    put = into(wide, list(range(count - 1)))
    for n in range(0, SIDE, BLOCK):
        shaped = [taps_ref[pl.ds(count * n + k, BLOCK, stride=count), :] * sign for k in range(1, count)]
        for r in range(2):
            frame = [late[0, r, t, pl.ds(n, BLOCK), :].astype(jnp.float32) for t in range(count - 1)]
            for t in range(count - 1):
                value = sums_ref[r, t, pl.ds(n, BLOCK), :]
                for k in range(t + 1, count):
                    value = value + shaped[k - 1] * frame[t - k + count - 1]
                put(r, n, t, value)
    return power_of(ins, wide, tall, count - 1)


def lay_out(every, apart, peers, step, start):
    for j in range(8):
        apart[pl.ds(start + j, peers, stride=step), :] = every[pl.ds(8 + j, peers, stride=8), :]
    lane = lax.broadcasted_iota(jnp.int32, (peers, SIDE), 1)
    after = every[pl.ds(16, peers, stride=8), :]
    before = every[pl.ds(7, peers, stride=8), :]
    apart[pl.ds(start + 8, peers, stride=step), :] = jnp.where(lane < SIDE // 2, after, before)


def ends(every, before, after):
    count = every.shape[0]
    every[pl.ds(0, 8), :] = before
    every[pl.ds(count - 8, 8), :] = after


def ship_kernel(p0, p1, p2, p3, border, out_ref):
    half = lax.axis_index("half")
    zero = jnp.zeros((8, SIDE), jnp.float32)
    before = jnp.where(half == 0, border[pl.ds(SIDE - 8, 8), :], zero)
    after = jnp.where(half == 1, border[pl.ds(0, 8), :], zero)
    out_ref[pl.ds(0, 16), :] = jnp.concatenate([zero, before], axis=0).astype(jnp.bfloat16)
    for i, ref in enumerate((p0, p1, p2, p3)):
        out_ref[pl.ds(16 + i * SIDE, SIDE), :] = ref[...].astype(jnp.bfloat16)
    out_ref[pl.ds(16 + 4 * SIDE, 16), :] = jnp.concatenate([after, zero], axis=0).astype(jnp.bfloat16)


def lay_kernel(p0, p3, border, p5, p6, theirs, relayed, out_ref, every, plain):
    half = lax.axis_index("half")
    peers = (out_ref.shape[0] - SPARE) // (2 * SENT)
    plain[...] = theirs[...].astype(jnp.float32) + relayed[...].astype(jnp.float32)
    lay_out(plain.at[pl.ds(8, plain.shape[0] - 16)], out_ref, peers, 2 * SENT, SENT)

    def put(slot, value):
        every[pl.ds(pl.multiple_of(8 + slot * SIDE, 8), SIDE), :] = value

    put(3 * (1 - half), border[...])
    put(half, p5[...])
    put(1 + half, p6[...])
    put(2 + half, jnp.zeros((SIDE, SIDE), jnp.float32))
    zero = jnp.zeros((8, SIDE), jnp.float32)
    ends(
        every,
        jnp.where(half == 1, p3[pl.ds(SIDE - 8, 8), :], zero),
        jnp.where(half == 0, p0[pl.ds(0, 8), :], zero),
    )
    lay_out(every, out_ref, peers, 2 * SENT, 0)


def last_kernel(*refs):
    ins, (late, part, sums_ref, border, p6, laid), out_ref, same_ref = refs[:6], refs[6:12], refs[12], refs[13]
    wide, tall, every = refs[14:]
    half = lax.axis_index("half")
    value = (part[...] + late_power(ins, late, sums_ref, wide, tall)).T
    every[pl.ds(8, SIDE), :] = value
    zero = jnp.zeros((8, SIDE), jnp.float32)
    ends(every, p6[pl.ds(SIDE - 8, 8), :], jnp.where(half == 0, border[pl.ds(0, 8), :], zero))
    group = SIDE // 8
    stride = 2 * SENT
    start = group * stride * (2 + half)
    lay_out(every, same_ref, group, stride, start)
    lane = lax.broadcasted_iota(jnp.int32, (1, SIDE), 1)
    row = pl.ds(start - stride + 8, 1)
    same_ref[row, :] = jnp.where(lane < SIDE // 2, value[:1], same_ref[row, :])

    @pl.when(half == 0)
    def _():
        row = pl.ds(3 * group * stride + 8, 1)
        same_ref[row, :] = jnp.where(lane < SIDE // 2, same_ref[row, :], value[SIDE - 1 :])

    out_ref[...] = same_ref[pl.ds(0, out_ref.shape[0]), :].astype(jnp.bfloat16)


def tree_kernel(scale, in_ref, out_ref, wide, steps, flat):
    half = lax.axis_index("half")
    step = 2 * SENT
    sources = in_ref.shape[0] // step
    per = sources // (NT // 2)
    lane = lax.broadcasted_iota(jnp.int32, (8, SIDE), 1)
    wide[pl.ds(0, in_ref.shape[0]), :] = in_ref[...].astype(jnp.float32)
    for whose in range(2):
        base = 8 * ROOM * (half if whose == 0 else 1 - half)
        for j in range(SENT):
            value = wide[pl.ds(whose * SENT + j, 8, stride=step * per), :]
            for i in range(1, per):
                value = value + wide[pl.ds(step * i + whose * SENT + j, 8, stride=step * per), :]
            for row in (8 + j,) if j < 8 else (7, 16):
                if whose == 0:
                    steps[pl.ds(base + row, 8, stride=ROOM), :] = value
                else:
                    steps[pl.ds(base + 6 * ROOM + row, 2, stride=ROOM), :] = value[:2]
                    steps[pl.ds(base + row, 6, stride=ROOM), :] = value[2:]

    def moved(value, move, sense):
        if move == 0:
            return value
        own, beside = value
        by = SIDE - move if sense > 0 else move
        mixed = jnp.where(lane < move if sense > 0 else lane >= SIDE - move, beside, own)
        return pltpu.roll(mixed, by, 1), pltpu.roll(beside, by, 1)

    senses = (1, -1)
    levels = [
        [[(steps[pl.ds(ROOM * s + 8, 8), :], steps[pl.ds(ROOM * s + 8 + sense, 8), :])] for s in range(NT)]
        for sense in senses
    ]
    length = 1
    while length < NT:
        nexts = [[], []]
        for j in range(0, len(levels[0]), 2):
            for level, following, sense in zip(levels, nexts, senses):
                following.append(
                    [
                        tuple(p + q for p, q in zip(level[j][d // 2], moved(level[j + 1][d // 2], d - d // 2, sense)))
                        for d in range(2 * length)
                    ]
                )
        levels = nexts
        length *= 2
    for which in range(2):
        for d in range(NT):
            flat[which, pl.ds(8 * d, 8), :] = levels[which][0][d][0]
    for which in range(2):
        for r in range(8):
            out_ref[which, :, pl.ds(r * SIDE, SIDE)] = flat[which, pl.ds(r, NT, stride=8), :] * scale


def call(body, name, args, shape, dtype, scratch, flops=1 << 20, after=(), specs=None, params=PARAMS, alias=None):
    several = isinstance(shape, list)

    def ordered(*refs):
        body(*refs[: len(args)], *refs[len(args) + len(after) :])

    return pl.pallas_call(
        ordered,
        in_specs=(specs or [VMEM] * len(args)) + [ANY] * len(after),
        out_specs=[VMEM] * len(shape) if several else VMEM,
        out_shape=[jax.ShapeDtypeStruct(*each) for each in shape] if several else jax.ShapeDtypeStruct(shape, dtype),
        scratch_shapes=scratch,
        input_output_aliases=alias or {},
        compiler_params=params,
        cost_estimate=pl.CostEstimate(flops=flops, bytes_accessed=1 << 20, transcendentals=0),
        name=name,
    )(*args, *after)


def bind(body, *first):
    def bound(*refs):
        body(*first, *refs)

    return bound


def per_device(voltages, taps):
    channels, _, _, frames, length = voltages.shape
    count = taps.shape[0]
    peers = lax.axis_size("tm")
    f32, bf16 = jnp.float32, jnp.bfloat16
    fourier, cos, sin = tables(SIDE)
    back = jnp.asarray(np.ascontiguousarray(fourier.T))
    fourier, cos, sin = jnp.asarray(fourier), jnp.asarray(cos), jnp.asarray(sin)
    rows = voltages.reshape(channels, 2, 2, frames, SIDE, SIDE).transpose(0, 1, 2, 4, 3, 5)
    rows = rows.reshape(channels, 2, 2, SIDE * frames, SIDE)
    coefficients = taps.reshape(count, SIDE, SIDE).transpose(1, 0, 2).reshape(SIDE * count, SIDE)
    pairs = [(i, i + 1) for i in range(2 * peers - 1)]
    tile = (SIDE, SIDE)

    halo = (2, 2, count - 1, SIDE, SIDE)
    interleaved = (SIDE * frames, SIDE)
    roomy = (SIDE * frames + 8, SIDE)
    first = call(
        first_pack_kernel,
        "pack_first",
        [rows],
        halo,
        bf16,
        [
            pltpu.VMEM((2, 2) + interleaved, bf16),
            pltpu.VMEM((2, 2) + roomy, f32),
            pltpu.SemaphoreType.DMA((2, 2)),
        ],
        specs=[ANY],
        params=FIRST,
    )
    packs = [first]
    near = [[lax.ppermute(first, ("half", "tm"), pairs)]] + [[] for _ in range(channels - 1)]

    def send(place, pols, after):
        shape = (len(pols),) + halo[1:]
        body = bind(pack_kernel, place, pols)
        value = call(body, "pack", [rows], shape, bf16, [pltpu.VMEM((2,) + roomy, f32)], after=after)
        packs.append(value)
        near[place].append(lax.ppermute(value, ("half", "tm"), pairs))

    constants = [coefficients, fourier, back, cos, sin]
    scratch = [
        pltpu.VMEM((2,) + roomy, f32),
        pltpu.VMEM((2 * SIDE, frames * SIDE), bf16),
        pltpu.VMEM((frames * SIDE, 2 * SIDE), bf16),
    ]
    flops = 300 << 20
    for place in range(1, AHEAD):
        send(place, (0, 1), [first])
    plane = 2 * peers // channels
    shipped = (16 + channels // 2 * SIDE + 16, SIDE)
    across, edge = [], (channels // 2 - 1) * plane + plane - 1
    for i in range(2 * peers):
        half, at = divmod(i, peers)
        across.append((i, (1 - half) * peers + (at + plane) % peers))
    straight = [pair for pair in across if pair[0] != edge]
    target = dict(across)[edge]
    beside = edge - 4
    power = []
    last = channels - 1
    for place in range(last):
        args = [rows, *constants, *near[place]]
        order = power[-1:] + ([theirs, by] if place == last - 2 else [])
        body = bind(chunk_kernel, place)
        power.append(call(body, "chunk", args, tile, f32, scratch, flops, after=order))
        if place == channels // 2:
            ship = call(ship_kernel, "ship", power[:5], shipped, bf16, [], after=[packs[-1]])
            theirs = lax.ppermute(ship, ("half", "tm"), straight)
            by = lax.ppermute(ship, ("half", "tm"), [(edge, beside)])
            relayed = lax.ppermute(by, ("half", "tm"), [(beside, target)])
        if place + AHEAD < last:
            send(place + AHEAD, (0, 1), power[-1:])
        elif place + AHEAD == last:
            send(last, (0,), power[-1:])
            send(last, (1,), power[-1:])
    sums = (2, count - 1) + tile
    part, begun = call(
        bind(early_kernel, last),
        "chunk_early",
        [rows, *constants, near[last][0]],
        [(tile, f32), (sums, f32)],
        None,
        scratch,
        flops,
        after=power[-1:],
    )
    sent = (2 * peers * SENT, SIDE)
    laid = call(
        lay_kernel,
        "lay",
        [power[0], power[3], *power[4:7], theirs, relayed],
        (sent[0] + SPARE, SIDE),
        f32,
        [pltpu.VMEM((8 + 4 * SIDE + 8, SIDE), f32), pltpu.VMEM(shipped, f32)],
        after=[part],
    )
    out, _ = call(
        last_kernel,
        "last",
        [rows, *constants, near[last][1], part, begun, power[4], power[6], laid],
        [(sent, bf16), ((sent[0] + SPARE, SIDE), f32)],
        None,
        scratch[1:] + [pltpu.VMEM((8 + SIDE + 8, SIDE), f32)],
        flops // 2,
        alias={11: 1},
    )
    out = out.reshape(peers, SENT, 2, SIDE)
    owned = lax.all_to_all(out, "tm", split_axis=0, concat_axis=0, tiled=True).reshape(sent)
    scale = 1.0 / (frames * 2 * peers)
    return call(
        bind(tree_kernel, scale),
        "tree",
        [owned],
        (2, NT, channels * length // (2 * peers)),
        f32,
        [
            pltpu.VMEM((sent[0] + 16 * SENT, SIDE), f32),
            pltpu.VMEM((ROOM * NT + ROOM, SIDE), f32),
            pltpu.VMEM((2, 8 * NT + 8, SIDE), f32),
        ],
    )


def solution(mesh):
    peers, groups = mesh.shape["tm"], mesh.shape["chan"]
    halves = Mesh(mesh.devices.reshape(2, peers // 2, groups), ("half", "tm", "chan"))
    split = ("half", "tm")
    placed = (P("chan", None, None, split, None), P())
    return jax.shard_map(per_device, mesh=halves, in_specs=placed, out_specs=P("chan", None, split), check_vma=False)
```

```python
import math

import jax
import jax.numpy as jnp
import ml_dtypes
import numpy as np
from jax import lax
from jax.experimental import pallas as pl
from jax.experimental.pallas import tpu as pltpu
from jax.sharding import Mesh
from jax.sharding import PartitionSpec as P

NT = 16
SIDE = 128
BLOCK = 16
AHEAD = 4
SENT = 9
SPARE = 24
ROOM = 24
PARAMS = pltpu.CompilerParams(vmem_limit_bytes=12 << 20)
FIRST = pltpu.CompilerParams(vmem_limit_bytes=56_000_000)
VMEM = pl.BlockSpec(memory_space=pltpu.VMEM)
ANY = pl.BlockSpec(memory_space=pl.ANY)


def tables(side):
    index = np.arange(side, dtype=np.int64)
    angle = -2.0 * math.pi / side * ((index[:, None] * index[None, :]) % side)
    re = (np.cos(angle) / math.sqrt(side)).astype(ml_dtypes.bfloat16)
    im = (np.sin(angle) / math.sqrt(side)).astype(ml_dtypes.bfloat16)
    fourier = np.block([[re, -im], [im, re]])
    turn = -2.0 * math.pi / (side * side) * (index[:, None] * index[None, :])
    return fourier, np.cos(turn).astype(np.float32), np.sin(turn).astype(np.float32)


def channel_at(place, half):
    lower = place + 4 if place < 4 else 3 if place == 4 else place - 5
    return lower + half * (place - lower)


def receiver_half():
    half, last = lax.axis_index("half"), lax.axis_size("tm") - 1
    return jnp.where((half == 0) & (lax.axis_index("tm") == last), 1, half)


def spread(value, rows, out_ref, p, r):
    frames = value.shape[0] // SIDE
    rows[pl.ds(0, value.shape[0]), :] = value.astype(jnp.float32)
    for t in range(1, frames):
        out_ref[p, r, t - 1] = rows[pl.ds(t, SIDE, stride=frames), :].astype(jnp.bfloat16)


def first_pack_kernel(v_ref, out_ref, block, rows, sems):
    channel = channel_at(0, receiver_half())
    copies = {}
    for p in range(2):
        for r in range(2):
            copies[p, r] = pltpu.make_async_copy(v_ref.at[channel, p, r], block.at[p, r], sems.at[p, r])
            copies[p, r].start()
    for p in range(2):
        for r in range(2):
            copies[p, r].wait()
            spread(block[p, r], rows.at[p, r], out_ref, p, r)


def pack_kernel(place, pols, v_ref, out_ref, rows):
    channel = channel_at(place, receiver_half())
    for i, p in enumerate(pols):
        for r in range(2):
            spread(v_ref[channel, p, r], rows.at[r], out_ref, i, r)


def filtered(ins, channel, p, halo, times, rows, put):
    v_ref, taps_ref = ins[:2]
    frames = v_ref.shape[3] // SIDE
    count = taps_ref.shape[0] // SIDE
    lane = lax.broadcasted_iota(jnp.int32, (BLOCK, SIDE), 1)
    sign = 1.0 - 2.0 * (lane % 2).astype(jnp.float32)
    for r in range(2):
        rows[r, pl.ds(0, frames * SIDE), :] = v_ref[channel, p, r].astype(jnp.float32)
    for n in range(0, SIDE, BLOCK):
        shaped = [taps_ref[pl.ds(count * n + k, BLOCK, stride=count), :] * sign for k in range(count)]
        for r in range(2):
            frame = {t: rows[r, pl.ds(frames * n + t, BLOCK, stride=frames), :] for t in range(max(times) + 1)}
            if halo is not None:
                for t in range(1 - count, 0):
                    frame[t] = halo[r, t + count - 1, pl.ds(n, BLOCK), :].astype(jnp.float32)
            for t in times:
                value = shaped[0] * frame[t]
                for k in range(1, count):
                    if t - k in frame:
                        value = value + shaped[k] * frame[t - k]
                put(r, n, t, value)


def into(wide, order):
    def put(r, n, t, value):
        wide[pl.ds(r * SIDE + n, BLOCK), pl.ds(order.index(t) * SIDE, SIDE)] = value.astype(jnp.bfloat16)

    return put


def power_of(ins, wide, tall, many):
    fourier_ref, back_ref, cos_ref, sin_ref = ins[2:]
    span = many * SIDE
    first = jnp.dot(fourier_ref[...], wide[:, pl.ds(0, span)], preferred_element_type=jnp.float32)
    cos, sin = cos_ref[...], sin_ref[...]
    for i in range(many):
        re = first[:SIDE, i * SIDE : (i + 1) * SIDE]
        im = first[SIDE:, i * SIDE : (i + 1) * SIDE]
        tall[pl.ds(i * SIDE, SIDE), pl.ds(0, SIDE)] = (re * cos - im * sin).astype(jnp.bfloat16)
        tall[pl.ds(i * SIDE, SIDE), pl.ds(SIDE, SIDE)] = (re * sin + im * cos).astype(jnp.bfloat16)
    spectrum = jnp.dot(tall[pl.ds(0, span), :], back_ref[...], preferred_element_type=jnp.float32)
    square = spectrum * spectrum
    total = None
    for i in range(many):
        part = square[i * SIDE : (i + 1) * SIDE]
        part = part[:, :SIDE] + part[:, SIDE:]
        total = part if total is None else total + part
    return total


def chunk_kernel(place, *refs):
    ins, near, out_ref, (rows, wide, tall) = refs[:6], refs[6], refs[7], refs[8:]
    channel = channel_at(place, lax.axis_index("half"))
    times = list(range(ins[0].shape[3] // SIDE))
    total = None
    for p in range(2):
        filtered(ins, channel, p, near.at[p], times, rows, into(wide, times))
        power = power_of(ins, wide, tall, len(times))
        total = power if total is None else total + power
    out_ref[...] = total.T


def early_kernel(place, *refs):
    ins, near, out_ref, sums_ref, (rows, wide, tall) = refs[:6], refs[6], refs[7], refs[8], refs[9:]
    channel = channel_at(place, lax.axis_index("half"))
    frames = ins[0].shape[3] // SIDE
    times = list(range(frames))
    filtered(ins, channel, 0, near.at[0], times, rows, into(wide, times))
    total = power_of(ins, wide, tall, frames)
    whole = into(wide, [frames - 1])

    def put(r, n, t, value):
        if t == frames - 1:
            whole(r, n, t, value)
        else:
            sums_ref[r, t, pl.ds(n, BLOCK), :] = value

    filtered(ins, channel, 1, None, times, rows, put)
    out_ref[...] = total + power_of(ins, wide, tall, 1)


def late_power(ins, late, sums_ref, wide, tall):
    taps_ref = ins[1]
    count = taps_ref.shape[0] // SIDE
    lane = lax.broadcasted_iota(jnp.int32, (BLOCK, SIDE), 1)
    sign = 1.0 - 2.0 * (lane % 2).astype(jnp.float32)
    put = into(wide, list(range(count - 1)))
    for n in range(0, SIDE, BLOCK):
        shaped = [taps_ref[pl.ds(count * n + k, BLOCK, stride=count), :] * sign for k in range(1, count)]
        for r in range(2):
            frame = [late[0, r, t, pl.ds(n, BLOCK), :].astype(jnp.float32) for t in range(count - 1)]
            for t in range(count - 1):
                value = sums_ref[r, t, pl.ds(n, BLOCK), :]
                for k in range(t + 1, count):
                    value = value + shaped[k - 1] * frame[t - k + count - 1]
                put(r, n, t, value)
    return power_of(ins, wide, tall, count - 1)


def lay_out(every, apart, peers, step, start):
    for j in range(8):
        apart[pl.ds(start + j, peers, stride=step), :] = every[pl.ds(8 + j, peers, stride=8), :]
    lane = lax.broadcasted_iota(jnp.int32, (peers, SIDE), 1)
    after = every[pl.ds(16, peers, stride=8), :]
    before = every[pl.ds(7, peers, stride=8), :]
    apart[pl.ds(start + 8, peers, stride=step), :] = jnp.where(lane < SIDE // 2, after, before)


def ends(every, before, after):
    count = every.shape[0]
    every[pl.ds(0, 8), :] = before
    every[pl.ds(count - 8, 8), :] = after


def ship_kernel(p0, p1, p2, p3, border, out_ref):
    half = lax.axis_index("half")
    zero = jnp.zeros((8, SIDE), jnp.float32)
    before = jnp.where(half == 0, border[pl.ds(SIDE - 8, 8), :], zero)
    after = jnp.where(half == 1, border[pl.ds(0, 8), :], zero)
    out_ref[pl.ds(0, 16), :] = jnp.concatenate([zero, before], axis=0).astype(jnp.bfloat16)
    for i, ref in enumerate((p0, p1, p2, p3)):
        out_ref[pl.ds(16 + i * SIDE, SIDE), :] = ref[...].astype(jnp.bfloat16)
    out_ref[pl.ds(16 + 4 * SIDE, 16), :] = jnp.concatenate([after, zero], axis=0).astype(jnp.bfloat16)


def lay_kernel(p0, p3, border, p5, p6, theirs, relayed, out_ref, every, plain):
    half = lax.axis_index("half")
    peers = (out_ref.shape[0] - SPARE) // (2 * SENT)
    plain[...] = theirs[...].astype(jnp.float32) + relayed[...].astype(jnp.float32)
    lay_out(plain.at[pl.ds(8, plain.shape[0] - 16)], out_ref, peers, 2 * SENT, SENT)

    def put(slot, value):
        every[pl.ds(pl.multiple_of(8 + slot * SIDE, 8), SIDE), :] = value

    put(3 * (1 - half), border[...])
    put(half, p5[...])
    put(1 + half, p6[...])
    put(2 + half, jnp.zeros((SIDE, SIDE), jnp.float32))
    zero = jnp.zeros((8, SIDE), jnp.float32)
    ends(
        every,
        jnp.where(half == 1, p3[pl.ds(SIDE - 8, 8), :], zero),
        jnp.where(half == 0, p0[pl.ds(0, 8), :], zero),
    )
    lay_out(every, out_ref, peers, 2 * SENT, 0)


def last_kernel(*refs):
    ins, (late, part, sums_ref, border, p6, laid), out_ref, same_ref = refs[:6], refs[6:12], refs[12], refs[13]
    wide, tall, every = refs[14:]
    half = lax.axis_index("half")
    settled = SIDE // 8 * 2 * SENT * 2 - 16
    out_ref[pl.ds(0, settled), :] = same_ref[pl.ds(0, settled), :].astype(jnp.bfloat16)
    value = (part[...] + late_power(ins, late, sums_ref, wide, tall)).T
    every[pl.ds(8, SIDE), :] = value
    zero = jnp.zeros((8, SIDE), jnp.float32)
    ends(every, p6[pl.ds(SIDE - 8, 8), :], jnp.where(half == 0, border[pl.ds(0, 8), :], zero))
    group = SIDE // 8
    stride = 2 * SENT
    start = group * stride * (2 + half)
    lay_out(every, same_ref, group, stride, start)
    lane = lax.broadcasted_iota(jnp.int32, (1, SIDE), 1)
    row = pl.ds(start - stride + 8, 1)
    same_ref[row, :] = jnp.where(lane < SIDE // 2, value[:1], same_ref[row, :])

    @pl.when(half == 0)
    def _():
        row = pl.ds(3 * group * stride + 8, 1)
        same_ref[row, :] = jnp.where(lane < SIDE // 2, same_ref[row, :], value[SIDE - 1 :])

    rest = pl.ds(settled, out_ref.shape[0] - settled)
    out_ref[rest, :] = same_ref[rest, :].astype(jnp.bfloat16)


def tree_kernel(scale, in_ref, out_ref, wide, steps, flat):
    half = lax.axis_index("half")
    step = 2 * SENT
    sources = in_ref.shape[0] // step
    per = sources // (NT // 2)
    lane = lax.broadcasted_iota(jnp.int32, (8, SIDE), 1)
    wide[pl.ds(0, in_ref.shape[0]), :] = in_ref[...].astype(jnp.float32)
    for whose in range(2):
        base = 8 * ROOM * (half if whose == 0 else 1 - half)
        for j in range(SENT):
            value = wide[pl.ds(whose * SENT + j, 8, stride=step * per), :]
            for i in range(1, per):
                value = value + wide[pl.ds(step * i + whose * SENT + j, 8, stride=step * per), :]
            for row in (8 + j,) if j < 8 else (7, 16):
                if whose == 0:
                    steps[pl.ds(base + row, 8, stride=ROOM), :] = value
                else:
                    steps[pl.ds(base + 6 * ROOM + row, 2, stride=ROOM), :] = value[:2]
                    steps[pl.ds(base + row, 6, stride=ROOM), :] = value[2:]

    def moved(value, move, sense):
        if move == 0:
            return value
        own, beside = value
        by = SIDE - move if sense > 0 else move
        mixed = jnp.where(lane < move if sense > 0 else lane >= SIDE - move, beside, own)
        return pltpu.roll(mixed, by, 1), pltpu.roll(beside, by, 1)

    senses = (1, -1)
    levels = [
        [[(steps[pl.ds(ROOM * s + 8, 8), :], steps[pl.ds(ROOM * s + 8 + sense, 8), :])] for s in range(NT)]
        for sense in senses
    ]
    length = 1
    while length < NT:
        nexts = [[], []]
        for j in range(0, len(levels[0]), 2):
            for level, following, sense in zip(levels, nexts, senses):
                following.append(
                    [
                        tuple(p + q for p, q in zip(level[j][d // 2], moved(level[j + 1][d // 2], d - d // 2, sense)))
                        for d in range(2 * length)
                    ]
                )
        levels = nexts
        length *= 2
    for which in range(2):
        for d in range(NT):
            flat[which, pl.ds(8 * d, 8), :] = levels[which][0][d][0]
    for which in range(2):
        for r in range(8):
            out_ref[which, :, pl.ds(r * SIDE, SIDE)] = flat[which, pl.ds(r, NT, stride=8), :] * scale


def call(body, name, args, shape, dtype, scratch, flops=1 << 20, after=(), specs=None, params=PARAMS, alias=None):
    several = isinstance(shape, list)

    def ordered(*refs):
        body(*refs[: len(args)], *refs[len(args) + len(after) :])

    return pl.pallas_call(
        ordered,
        in_specs=(specs or [VMEM] * len(args)) + [ANY] * len(after),
        out_specs=[VMEM] * len(shape) if several else VMEM,
        out_shape=[jax.ShapeDtypeStruct(*each) for each in shape] if several else jax.ShapeDtypeStruct(shape, dtype),
        scratch_shapes=scratch,
        input_output_aliases=alias or {},
        compiler_params=params,
        cost_estimate=pl.CostEstimate(flops=flops, bytes_accessed=1 << 20, transcendentals=0),
        name=name,
    )(*args, *after)


def bind(body, *first):
    def bound(*refs):
        body(*first, *refs)

    return bound


def per_device(voltages, taps):
    channels, _, _, frames, length = voltages.shape
    count = taps.shape[0]
    peers = lax.axis_size("tm")
    f32, bf16 = jnp.float32, jnp.bfloat16
    fourier, cos, sin = tables(SIDE)
    back = jnp.asarray(np.ascontiguousarray(fourier.T))
    fourier, cos, sin = jnp.asarray(fourier), jnp.asarray(cos), jnp.asarray(sin)
    rows = voltages.reshape(channels, 2, 2, frames, SIDE, SIDE).transpose(0, 1, 2, 4, 3, 5)
    rows = rows.reshape(channels, 2, 2, SIDE * frames, SIDE)
    coefficients = taps.reshape(count, SIDE, SIDE).transpose(1, 0, 2).reshape(SIDE * count, SIDE)
    pairs = [(i, i + 1) for i in range(2 * peers - 1)]
    tile = (SIDE, SIDE)

    halo = (2, 2, count - 1, SIDE, SIDE)
    interleaved = (SIDE * frames, SIDE)
    roomy = (SIDE * frames + 8, SIDE)
    first = call(
        first_pack_kernel,
        "pack_first",
        [rows],
        halo,
        bf16,
        [
            pltpu.VMEM((2, 2) + interleaved, bf16),
            pltpu.VMEM((2, 2) + roomy, f32),
            pltpu.SemaphoreType.DMA((2, 2)),
        ],
        specs=[ANY],
        params=FIRST,
    )
    packs = [first]
    near = [[lax.ppermute(first, ("half", "tm"), pairs)]] + [[] for _ in range(channels - 1)]

    def send(place, pols, after):
        shape = (len(pols),) + halo[1:]
        body = bind(pack_kernel, place, pols)
        value = call(body, "pack", [rows], shape, bf16, [pltpu.VMEM((2,) + roomy, f32)], after=after)
        packs.append(value)
        near[place].append(lax.ppermute(value, ("half", "tm"), pairs))

    constants = [coefficients, fourier, back, cos, sin]
    scratch = [
        pltpu.VMEM((2,) + roomy, f32),
        pltpu.VMEM((2 * SIDE, frames * SIDE), bf16),
        pltpu.VMEM((frames * SIDE, 2 * SIDE), bf16),
    ]
    flops = 300 << 20
    for place in range(1, AHEAD):
        send(place, (0, 1), [first])
    plane = 2 * peers // channels
    shipped = (16 + channels // 2 * SIDE + 16, SIDE)
    across, edge = [], (channels // 2 - 1) * plane + plane - 1
    for i in range(2 * peers):
        half, at = divmod(i, peers)
        across.append((i, (1 - half) * peers + (at + plane) % peers))
    straight = [pair for pair in across if pair[0] != edge]
    target = dict(across)[edge]
    beside = edge - 4
    power = []
    last = channels - 1
    for place in range(last):
        args = [rows, *constants, *near[place]]
        order = power[-1:] + ([theirs, by] if place == last - 2 else [])
        body = bind(chunk_kernel, place)
        power.append(call(body, "chunk", args, tile, f32, scratch, flops, after=order))
        if place == channels // 2:
            ship = call(ship_kernel, "ship", power[:5], shipped, bf16, [], after=[packs[-1]])
            theirs = lax.ppermute(ship, ("half", "tm"), straight)
            by = lax.ppermute(ship, ("half", "tm"), [(edge, beside)])
            relayed = lax.ppermute(by, ("half", "tm"), [(beside, target)])
        if place + AHEAD < last:
            send(place + AHEAD, (0, 1), power[-1:])
        elif place + AHEAD == last:
            send(last, (0,), power[-1:])
            send(last, (1,), power[-1:])
    sums = (2, count - 1) + tile
    part, begun = call(
        bind(early_kernel, last),
        "chunk_early",
        [rows, *constants, near[last][0]],
        [(tile, f32), (sums, f32)],
        None,
        scratch,
        flops,
        after=power[-1:],
    )
    sent = (2 * peers * SENT, SIDE)
    laid = call(
        lay_kernel,
        "lay",
        [power[0], power[3], *power[4:7], theirs, relayed],
        (sent[0] + SPARE, SIDE),
        f32,
        [pltpu.VMEM((8 + 4 * SIDE + 8, SIDE), f32), pltpu.VMEM(shipped, f32)],
        after=[part],
    )
    out, _ = call(
        last_kernel,
        "last",
        [rows, *constants, near[last][1], part, begun, power[4], power[6], laid],
        [(sent, bf16), ((sent[0] + SPARE, SIDE), f32)],
        None,
        scratch[1:] + [pltpu.VMEM((8 + SIDE + 8, SIDE), f32)],
        flops // 2,
        alias={11: 1},
    )
    out = out.reshape(peers, SENT, 2, SIDE)
    owned = lax.all_to_all(out, "tm", split_axis=0, concat_axis=0, tiled=True).reshape(sent)
    scale = 1.0 / (frames * 2 * peers)
    return call(
        bind(tree_kernel, scale),
        "tree",
        [owned],
        (2, NT, channels * length // (2 * peers)),
        f32,
        [
            pltpu.VMEM((sent[0] + 16 * SENT, SIDE), f32),
            pltpu.VMEM((ROOM * NT + ROOM, SIDE), f32),
            pltpu.VMEM((2, 8 * NT + 8, SIDE), f32),
        ],
    )


def solution(mesh):
    peers, groups = mesh.shape["tm"], mesh.shape["chan"]
    halves = Mesh(mesh.devices.reshape(2, peers // 2, groups), ("half", "tm", "chan"))
    split = ("half", "tm")
    placed = (P("chan", None, None, split, None), P())
    return jax.shard_map(per_device, mesh=halves, in_specs=placed, out_specs=P("chan", None, split), check_vma=False)
```
